128 devices in a mesh: kr: 8 (over x, z_lo), kc: 16 (over z_hi, y, core).
Axes of the slice: x: 4, y: 4, z: 4 (z_hi: 2, z_lo: 2; z = z_hi * 2 + z_lo), core: 2. Of those that a mesh axis runs over, the one named last changes fastest.
Arguments:
- densities: bfloat16 [128, 64, 2048], P('kc', None, 'kr'), may hold values from -0.890625 to 0.890625
- screened: bfloat16 [16, 2048, 2048], P(None, 'kr', 'kc'), may hold values from -1 to 3, as said below
- q_table: int32 [128, 128], replicated, may hold values from 0 to 15, as said below
Outputs:
- kernel: float32 [8192, 8192], P('kr', 'kc')
The draws below stay inside these ranges and needn't reach their ends.
Inputs may be any that keep to these rules, and one draw needn't show every extreme that they name: screened is symmetric in its last two dimensions. q_table[k, k'] = (pos[k] - pos[k']) mod 16 for integer grid positions pos of the k points.
All inputs are finite; a program needn't handle non-finite values.
Results may differ from the reference program's by a relative error of at most 0.0025.
Values may be sent and summed in bfloat16 or wider, within the bound.
A program may use at most 128 MiB of HBM per device.

```python
import math
import jax
import jax.numpy as jnp
from jax import lax

NP = 64
NG = 2048
NQ = 16
KB = 8
NK = 128
N_KC = 16


def draw_screened(key, part):
    key = jax.random.fold_in(key, 11)
    key_spread, key_diagonal = jax.random.split(key)
    spread = jnp.clip(jax.random.normal(key_spread, (NQ, NG, NG), jnp.float32), -5.0, 5.0)
    spread = (spread + jnp.swapaxes(spread, 1, 2)) * (0.5 / math.sqrt(NG))
    diagonal_part = jnp.exp(jax.random.uniform(key_diagonal, (NQ, NG), jnp.float32, math.log(0.5), math.log(2.0)))
    identity = jnp.eye(NG, dtype=jnp.float32)
    return (spread + diagonal_part[:, :, None] * identity).astype(jnp.bfloat16)


def draw_q_table(key, part):
    key = jax.random.fold_in(key, 23)
    places = jax.random.randint(key, (NK,), 0, NQ)
    places = places.at[0].set(0).at[1].set(1)
    return jnp.mod(places[:, None] - places[None, :], NQ).astype(jnp.int32)


def level_of(stream_key, shape, cuts, least, top_value):
    loudness, own = 1.0, jax.random.fold_in(stream_key, 6)
    for axis_at, parts in cuts:
        heights = jnp.exp(jax.random.uniform(jax.random.fold_in(own, axis_at), (parts,), jnp.float32, least / len(cuts), top_value / len(cuts)))
        loudness = loudness * jnp.repeat(heights, shape[axis_at] // parts).reshape([-1 if axis == axis_at else 1 for axis in range(len(shape))])
    return loudness


def scatter_about(rng, extent, scale, reach, cuts=(), held_as=jnp.bfloat16):
    array = scale * jax.random.normal(rng, extent, jnp.float32)
    if cuts:
        array = array * level_of(rng, extent, cuts, -0.22, 0.18)
    return jnp.clip(array, -reach, reach).astype(held_as)


def setup_inputs(seed: int = 0) -> dict:
    key_of = jax.random.split(jax.random.key(seed), 4)
    return {
        "densities": scatter_about(key_of[0], (NK, NP, NG), (NG ** -0.25), 0.890625, ((0, 16), (2, 8))),
        "screened": draw_screened(jax.random.fold_in(key_of[3], 71), 0),
        "q_table": draw_q_table(jax.random.fold_in(key_of[3], 71), 0),
    }


def reference(densities, screened, q_table):
    k_total = densities.shape[0]
    dens_wide = densities.astype(jnp.float32)
    screen_wide = screened.astype(jnp.float32)
    picker = jnp.arange(KB).astype(jnp.int32)[None, :]
    block_of = jnp.arange(k_total).astype(jnp.int32) // KB

    def column(col_index):
        col_dens = lax.dynamic_slice_in_dim(dens_wide, (col_index * KB).astype(jnp.int32), KB, 0)
        y_cols = jnp.einsum("qgh,jph->qjpg", screen_wide, col_dens)
        y_round = lax.optimization_barrier(y_cols.astype(jnp.bfloat16)).astype(jnp.float32)
        q_columns = lax.dynamic_slice_in_dim(q_table, (col_index * KB).astype(jnp.int32), KB, 1)
        chosen = y_round[q_columns, picker]
        partial_value = jnp.einsum("kpg,kjrg->kpjr", dens_wide, chosen)
        live = (block_of <= col_index).astype(jnp.float32)
        return (partial_value * live[:, None, None, None]).reshape(k_total * NP, KB * NP)

    slabs = lax.map(column, jnp.arange(N_KC).astype(jnp.int32))
    return jnp.transpose(slabs, (1, 0, 2)).reshape(k_total * NP, N_KC * KB * NP)
```

```python
import functools

import jax
import jax.numpy as jnp
from jax import lax
from jax.experimental import pallas as pl
from jax.experimental.pallas import tpu as pltpu
from jax.sharding import PartitionSpec as P

MESH = pl.DeviceIdType.MESH
NT = (((1,), (1,)), ((), ()))
CHUNKS = 4
KINDS = 16


def kernel(d_ref, w_ref, q_ref, out_ref, wb, drow, dcol, dtmp, yb, psend, zrecv, xsend, xrecv, ssend, srecv,
           loc_sem, a_send, a_recv, d_send, d_recv, z_send, z_recv, x_send, x_recv, s_send, s_recv):
    r, c = lax.axis_index("kr"), lax.axis_index("kc")
    x, zl = r // 2, r % 2
    zh, y, core = c // 8, (c // 2) % 4, c % 2
    q_count = w_ref.shape[0]
    per = q_count // CHUNKS
    odd = core == 1
    vc = jnp.where(odd, 16 - c, c)
    swap_c = jnp.where(odd, 16 - c, c)

    def cid(zh_, y_, core_):
        return zh_ * 8 + y_ * 2 + core_

    yp, ym, y2, zo = (y + 1) % 4, (y + 3) % 4, (y + 2) % 4, 1 - zh
    up, down, across, sib = (r, cid(zh, yp, core)), (r, cid(zh, ym, core)), (r, cid(zo, y, core)), (r, cid(zh, y, 1 - core))

    def plane(i):
        return (r + i) % 8

    barrier = pltpu.get_barrier_semaphore()

    def greet(to):
        pl.semaphore_signal(barrier, inc=1, device_id=to, device_id_type=MESH)

    load_w = pltpu.make_async_copy(w_ref, wb.at[c], loc_sem.at[0])
    load_d = pltpu.make_async_copy(d_ref, drow.at[c], loc_sem.at[1])
    load_w.start()
    load_d.start()
    for to in (up, down, across, sib):
        greet(to)
    for i in range(1, 8):
        greet((plane(i), c))

    @pl.when(odd)
    def _():
        greet((r, swap_c))
        pl.semaphore_wait(barrier, 12)

    @pl.when(jnp.logical_not(odd))
    def _():
        pl.semaphore_wait(barrier, 11)

    load_d.wait()
    load_w.wait()

    def remote(src, dst, ssem, rsem, to):
        return pltpu.make_async_remote_copy(
            src_ref=src, dst_ref=dst, send_sem=ssem, recv_sem=rsem, device_id=to, device_id_type=MESH
        )

    swap_d = remote(drow.at[c], dtmp, d_send.at[0], d_recv.at[0], (r, swap_c))
    keep_d = pltpu.make_async_copy(drow.at[c], dtmp, loc_sem.at[2])

    @pl.when(odd)
    def _():
        swap_d.start()

    @pl.when(jnp.logical_not(odd))
    def _():
        keep_d.start()

    def part(s, who, half=None):
        if s < CHUNKS:
            if half is None:
                return wb.at[who, pl.ds(s * per, per)]
            return wb.at[who, pl.ds(s * per + half * (per // 2), per // 2)]
        if half is None:
            return drow.at[who]
        rows = drow.shape[1] // 2
        return drow.at[who, pl.ds(half * rows, rows)]

    sent = []

    def send(s, kind, who, to, recv_kind, half=None):
        ref = part(s, who, half)
        copy = remote(ref, ref, a_send.at[s, kind], a_recv.at[s, recv_kind], to)
        copy.start()
        sent.append(copy)

    def arrived(s, kind, who, half=None):
        ref = part(s, who, half)
        remote(ref, ref, a_send.at[s, kind], a_recv.at[s, kind], sib).wait_recv()

    c_ym, c_yp, c_y2 = cid(zh, ym, core), cid(zh, yp, core), cid(zh, y2, core)
    c_z, c_zym, c_zyp, c_zy2 = cid(zo, y, core), cid(zo, ym, core), cid(zo, yp, core), cid(zo, y2, core)
    blocks = [c, c_ym, c_yp, c_z, c_y2, c_zym, c_zyp, c_zy2]

    def own(s):
        send(s, 0, c, up, 0)
        send(s, 1, c, down, 1)
        send(s, 2, c, across, 2)
        send(s, 3, c, sib, 8)

    def relay_near(s):
        arrived(s, 0, c_ym)
        send(s, 4, c_ym, up, 3, 0)
        send(s, 5, c_ym, sib, 9)
        arrived(s, 1, c_yp)
        send(s, 6, c_yp, down, 4, 1)
        send(s, 7, c_yp, sib, 10)
        arrived(s, 2, c_z)
        send(s, 8, c_z, up, 5)
        send(s, 9, c_z, down, 6)
        send(s, 10, c_z, sib, 11)

    def relay_far(s):
        arrived(s, 3, c_y2, 0)
        arrived(s, 4, c_y2, 1)
        send(s, 11, c_y2, across, 7)
        send(s, 12, c_y2, sib, 12)

    def finish(s):
        arrived(s, 5, c_zym)
        send(s, 13, c_zym, sib, 13)
        arrived(s, 6, c_zyp)
        send(s, 14, c_zyp, sib, 14)
        arrived(s, 7, c_zy2)
        send(s, 15, c_zy2, sib, 15)
        for i, who in enumerate(blocks):
            arrived(s, 8 + i, who - core + (1 - core))

    def screen(s):
        def one(i, carry):
            q = s * per + i
            lhs = jnp.concatenate([dcol[j] for j in range(8)], axis=1)
            rhs = jnp.concatenate([wb[j, q] for j in range(16)], axis=1)
            yb[q] = lax.dot_general(lhs, rhs, NT, preferred_element_type=jnp.float32).astype(jnp.bfloat16)
            return carry

        lax.fori_loop(0, per, one, 0)

    for s in range(CHUNKS + 1):
        own(s)

    @pl.when(odd)
    def _():
        swap_d.wait()

    @pl.when(jnp.logical_not(odd))
    def _():
        keep_d.wait()

    col_copies = []
    for i in range(1, 8):
        copy = remote(dtmp, dcol.at[r], d_send.at[i], d_recv.at[i], (plane(i), c))
        copy.start()
        col_copies.append(copy)
    col_own = pltpu.make_async_copy(dtmp, dcol.at[r], loc_sem.at[3])
    col_own.start()

    relay_near(0)
    relay_near(1)
    relay_far(0)
    relay_near(2)
    relay_far(1)
    finish(0)
    col_own.wait()
    for i in range(1, 8):
        src = dcol.at[(r + 8 - i) % 8]
        remote(src, src, d_send.at[i], d_recv.at[i], sib).wait_recv()
    screen(0)
    relay_near(3)
    relay_far(2)
    finish(1)
    screen(1)
    relay_near(4)
    relay_far(3)
    finish(2)
    screen(2)
    relay_far(4)
    finish(3)
    screen(3)
    finish(4)

    def product(b, k):
        rhs = jnp.concatenate(
            [yb[q_ref[b * 8 + k, vc * 8 + j], pl.ds(j * 64, 64), :] for j in range(8)], axis=0
        )
        lhs = drow[b, pl.ds(k * 64, 64), :]
        return lax.dot_general(lhs, rhs, NT, preferred_element_type=jnp.float32)

    partner = (r - zl + (1 - zl), c)

    def row_block(t, zl_):
        x_to = (x + 1 + t // 2) % 4
        return 2 * (2 * x_to + zl_) + t % 2

    def z_copy(t):
        return remote(psend.at[t], zrecv.at[t], z_send.at[t], z_recv.at[t], partner)

    def to_partner(t, carry):
        b = row_block(t, 1 - zl)

        @pl.when(b <= vc)
        def _():
            for k in range(8):
                psend[t, pl.ds(k * 64, 64), :] = product(b, k).astype(jnp.bfloat16)
            z_copy(t).start()

        return carry

    lax.fori_loop(0, 8, to_partner, 0)

    def x_copy(t):
        x_to = (x + 1 + t // 2) % 4
        return remote(xsend.at[t], xrecv.at[t], x_send.at[t], x_recv.at[t], (2 * x_to + zl, c))

    def along_x(t, carry):
        b = row_block(t, zl)

        @pl.when(b <= vc)
        def _():
            z_copy(t).wait_recv()
            for k in range(8):
                rows = pl.ds(k * 64, 64)
                xsend[t, rows, :] = (product(b, k) + zrecv[t, rows, :].astype(jnp.float32)).astype(jnp.bfloat16)
            x_copy(t).start()

        return carry

    lax.fori_loop(0, 6, along_x, 0)

    def s_copy(i):
        return remote(ssend.at[i], srecv.at[i], s_send.at[i], s_recv.at[i], (r, swap_c))

    for i in range(2):
        b = 2 * r + i
        t = 6 + i

        @pl.when(b <= vc)
        def _():
            z_copy(t).wait_recv()
            for k in range(8):
                out_ref[pl.ds(i * 512 + k * 64, 64), :] = product(b, k) + zrecv[t, pl.ds(k * 64, 64), :].astype(jnp.float32)
            for e in range(3):
                x_copy(2 * e + i).wait_recv()

            @pl.when(odd)
            def _():
                for k in range(8):
                    rows = pl.ds(k * 64, 64)
                    total = out_ref[pl.ds(i * 512 + k * 64, 64), :]
                    for e in range(3):
                        total = total + xrecv[2 * e + i, rows, :].astype(jnp.float32)
                    ssend[i, rows, :] = total.astype(jnp.bfloat16)
                s_copy(i).start()

            @pl.when(jnp.logical_not(odd))
            def _():
                for k in range(8):
                    rows = pl.ds(k * 64, 64)
                    total = out_ref[pl.ds(i * 512 + k * 64, 64), :]
                    for e in range(3):
                        total = total + xrecv[2 * e + i, rows, :].astype(jnp.float32)
                    out_ref[pl.ds(i * 512 + k * 64, 64), :] = total

    for i in range(2):
        b = 2 * r + i

        @pl.when(b > c)
        def _():
            out_ref[pl.ds(i * 512, 512), :] = jnp.zeros((512, 512), jnp.float32)

        @pl.when(jnp.logical_and(odd, b <= c))
        def _():
            s_copy(i).wait_recv()
            out_ref[pl.ds(i * 512, 512), :] = srecv[i].astype(jnp.float32)

    for copy in sent + col_copies:
        copy.wait_send()

    def drain_z(t, carry):
        @pl.when(row_block(t, 1 - zl) <= vc)
        def _():
            z_copy(t).wait_send()

        return carry

    lax.fori_loop(0, 8, drain_z, 0)

    def drain_x(t, carry):
        @pl.when(row_block(t, zl) <= vc)
        def _():
            x_copy(t).wait_send()

        return carry

    lax.fori_loop(0, 6, drain_x, 0)
    for i in range(2):
        @pl.when(jnp.logical_and(odd, 2 * r + i <= vc))
        def _():
            s_copy(i).wait_send()


def local(densities, screened, q_table):
    block_len, pair_count, g_slice = densities.shape
    d = densities.reshape(block_len * pair_count, g_slice)
    bf = jnp.bfloat16
    dma = pltpu.SemaphoreType.DMA
    return pl.pallas_call(
        kernel,
        out_shape=jax.ShapeDtypeStruct((1024, 512), jnp.float32),
        in_specs=[
            pl.BlockSpec(memory_space=pl.ANY),
            pl.BlockSpec(memory_space=pl.ANY),
            pl.BlockSpec(memory_space=pltpu.SMEM),
        ],
        out_specs=pl.BlockSpec(memory_space=pltpu.VMEM),
        scratch_shapes=[
            pltpu.VMEM((16, 16, 256, 128), bf),
            pltpu.VMEM((16, 512, 256), bf),
            pltpu.VMEM((8, 512, 256), bf),
            pltpu.VMEM((512, 256), bf),
            pltpu.VMEM((16, 512, 256), bf),
            pltpu.VMEM((8, 512, 512), bf),
            pltpu.VMEM((8, 512, 512), bf),
            pltpu.VMEM((6, 512, 512), bf),
            pltpu.VMEM((6, 512, 512), bf),
            pltpu.VMEM((2, 512, 512), bf),
            pltpu.VMEM((2, 512, 512), bf),
            dma((4,)),
            dma((CHUNKS + 1, KINDS)),
            dma((CHUNKS + 1, KINDS)),
            dma((8,)),
            dma((8,)),
            dma((8,)),
            dma((8,)),
            dma((6,)),
            dma((6,)),
            dma((2,)),
            dma((2,)),
        ],
        compiler_params=pltpu.CompilerParams(
            collective_id=0, has_side_effects=True, vmem_limit_bytes=60 * 2**20
        ),
        cost_estimate=pl.CostEstimate(flops=10 * 10**9, bytes_accessed=4 * 2**20, transcendentals=0),
    )(d, screened, q_table)


def solution(mesh):
    return jax.shard_map(
        local,
        mesh=mesh,
        in_specs=(P("kc", None, "kr"), P(None, "kr", "kc"), P()),
        out_specs=P("kr", "kc"),
        check_vma=False,
    )
```

```python
import functools

import jax
import jax.numpy as jnp
from jax import lax
from jax.experimental import pallas as pl
from jax.experimental.pallas import tpu as pltpu
from jax.sharding import PartitionSpec as P

MESH = pl.DeviceIdType.MESH
NT = (((1,), (1,)), ((), ()))
CHUNKS = 4
KINDS = 16
AX, AZ, BZ, BX, BS, ITEMS = 0, 12, 16, 24, 30, 32


def kernel(d_ref, w_ref, q_ref, out_ref, wb, drow, dcol, dtmp, yb, pout, pin,
           loc_sem, a_send, a_recv, d_send, d_recv, p_send, p_recv):
    r, c = lax.axis_index("kr"), lax.axis_index("kc")
    x, zl = r // 2, r % 2
    zh, y, core = c // 8, (c // 2) % 4, c % 2
    q_count = w_ref.shape[0]
    per = q_count // CHUNKS
    odd = core == 1
    vc = jnp.where(odd, 16 - c, c)
    swap_c = jnp.where(odd, 16 - c, c)

    def cid(zh_, y_, core_):
        return zh_ * 8 + y_ * 2 + core_

    yp, ym, y2, zo = (y + 1) % 4, (y + 3) % 4, (y + 2) % 4, 1 - zh
    up, down, across, sib = (r, cid(zh, yp, core)), (r, cid(zh, ym, core)), (r, cid(zo, y, core)), (r, cid(zh, y, 1 - core))

    partner = (2 * x + 1 - zl, c)

    def along(i):
        return 2 * ((x + i) % 4) + zl

    barrier = pltpu.get_barrier_semaphore()

    def greet(to):
        pl.semaphore_signal(barrier, inc=1, device_id=to, device_id_type=MESH)

    load_w = pltpu.make_async_copy(w_ref, wb.at[c], loc_sem.at[0])
    load_d = pltpu.make_async_copy(d_ref, drow.at[c], loc_sem.at[1])
    load_w.start()
    load_d.start()
    for to in (up, down, across, sib, partner):
        greet(to)
    for i in range(1, 4):
        greet((along(i), c))

    @pl.when(odd)
    def _():
        greet((r, swap_c))
        greet((partner[0], swap_c))
        pl.semaphore_wait(barrier, 10)

    @pl.when(jnp.logical_not(odd))
    def _():
        pl.semaphore_wait(barrier, 8)

    load_d.wait()
    load_w.wait()

    def remote(src, dst, ssem, rsem, to):
        return pltpu.make_async_remote_copy(
            src_ref=src, dst_ref=dst, send_sem=ssem, recv_sem=rsem, device_id=to, device_id_type=MESH
        )

    swap_d = remote(drow.at[c], dtmp, d_send.at[7], d_recv.at[7], (r, swap_c))
    keep_d = pltpu.make_async_copy(drow.at[c], dtmp, loc_sem.at[2])

    @pl.when(odd)
    def _():
        swap_d.start()

    @pl.when(jnp.logical_not(odd))
    def _():
        keep_d.start()

    def part(s, who, half=None):
        if s < CHUNKS:
            if half is None:
                return wb.at[who, pl.ds(s * per, per)]
            return wb.at[who, pl.ds(s * per + half * (per // 2), per // 2)]
        if half is None:
            return drow.at[who]
        rows = drow.shape[1] // 2
        return drow.at[who, pl.ds(half * rows, rows)]

    sent = []

    def send(s, kind, who, to, recv_kind, half=None):
        ref = part(s, who, half)
        copy = remote(ref, ref, a_send.at[s, kind], a_recv.at[s, recv_kind], to)
        copy.start()
        sent.append(copy)

    def arrived(s, kind, who, half=None):
        ref = part(s, who, half)
        remote(ref, ref, a_send.at[s, kind], a_recv.at[s, kind], sib).wait_recv()

    c_ym, c_yp, c_y2 = cid(zh, ym, core), cid(zh, yp, core), cid(zh, y2, core)
    c_z, c_zym, c_zyp, c_zy2 = cid(zo, y, core), cid(zo, ym, core), cid(zo, yp, core), cid(zo, y2, core)
    blocks = [c, c_ym, c_yp, c_z, c_y2, c_zym, c_zyp, c_zy2]

    def own(s):
        send(s, 0, c, up, 0)
        send(s, 1, c, down, 1)
        send(s, 2, c, across, 2)
        send(s, 3, c, sib, 8)

    def relay_near(s):
        arrived(s, 0, c_ym)
        send(s, 4, c_ym, up, 3, 0)
        send(s, 5, c_ym, sib, 9)
        arrived(s, 1, c_yp)
        send(s, 6, c_yp, down, 4, 1)
        send(s, 7, c_yp, sib, 10)
        arrived(s, 2, c_z)
        send(s, 8, c_z, up, 5)
        send(s, 9, c_z, down, 6)
        send(s, 10, c_z, sib, 11)

    def relay_far(s):
        arrived(s, 3, c_y2, 0)
        arrived(s, 4, c_y2, 1)
        send(s, 11, c_y2, across, 7)
        send(s, 12, c_y2, sib, 12)

    def finish(s):
        arrived(s, 5, c_zym)
        send(s, 13, c_zym, sib, 13)
        arrived(s, 6, c_zyp)
        send(s, 14, c_zyp, sib, 14)
        arrived(s, 7, c_zy2)
        send(s, 15, c_zy2, sib, 15)
        for i, who in enumerate(blocks):
            arrived(s, 8 + i, who - core + (1 - core))

    def screen(s):
        def one(i, carry):
            q = s * per + i
            lhs = jnp.concatenate([dcol[j] for j in range(8)], axis=1)
            rhs = jnp.concatenate([wb[j, q] for j in range(16)], axis=1)
            yb[q] = lax.dot_general(lhs, rhs, NT, preferred_element_type=jnp.float32).astype(jnp.bfloat16)
            return carry

        lax.fori_loop(0, per, one, 0)

    for s in range(CHUNKS + 1):
        own(s)

    @pl.when(odd)
    def _():
        swap_d.wait()

    @pl.when(jnp.logical_not(odd))
    def _():
        keep_d.wait()

    col_copies = []

    def col_send(i, src, who, to):
        copy = remote(src, dcol.at[who], d_send.at[i], d_recv.at[i], to)
        copy.start()
        col_copies.append(copy)

    def col_arrived(i, who):
        src = dcol.at[who]
        remote(src, src, d_send.at[i], d_recv.at[i], sib).wait_recv()

    col_send(0, dtmp, r, partner)
    for i in range(1, 4):
        col_send(i, dtmp, r, (along(i), c))
    col_own = pltpu.make_async_copy(dtmp, dcol.at[r], loc_sem.at[3])
    col_own.start()

    col_arrived(0, partner[0])
    for i in range(1, 4):
        col_send(3 + i, dcol.at[partner[0]], partner[0], (along(i), c))
    relay_near(0)
    relay_near(1)
    relay_far(0)
    relay_near(2)
    relay_far(1)
    finish(0)
    col_own.wait()
    for i in range(1, 4):
        col_arrived(i, along(4 - i))
        col_arrived(3 + i, 2 * ((x + 4 - i) % 4) + 1 - zl)
    screen(0)
    relay_near(3)
    relay_far(2)
    finish(1)
    screen(1)
    relay_near(4)
    relay_far(3)
    finish(2)
    screen(2)
    relay_far(4)
    finish(3)
    screen(3)
    finish(4)

    def product(b, k, half):
        rhs = jnp.concatenate(
            [yb[q_ref[b * 8 + k, vc * 8 + j], pl.ds(j * 64, 64), :] for j in range(4 * half, 4 * half + 4)], axis=0
        )
        lhs = drow[b, pl.ds(k * 64, 64), :]
        return lax.dot_general(lhs, rhs, NT, preferred_element_type=jnp.float32)

    step = 1 - 2 * (x % 2)
    x_far, x_pair, x_next = (x + 2) % 4, (x + 4 + step) % 4, (x + 4 - step) % 4
    to_pair, to_next = (2 * x_pair + zl, c), (2 * x_next + zl, c)
    dest = [x_far, x_pair, x_next, x]

    def a_row(role, i):
        return 4 * dest[role] + i

    def b_row(role, i, zl_):
        return 4 * dest[role] + 2 * zl_ + i

    def item(base, i, to):
        return remote(pout.at[base + i], pin.at[base + i], p_send.at[base + i], p_recv.at[base + i], to)

    def fill(base, i, b, half, adds):
        for k in range(8):
            rows = pl.ds(k * 64, 64)
            value = product(b, k, half)
            for add in adds:
                value = value + pin[add, rows, :].astype(jnp.float32)
            pout[base + i, rows, :] = value.astype(jnp.bfloat16)

    def each(count, row, body):
        def one(i, carry):
            b = row(i)

            @pl.when(b <= vc)
            def _():
                body(i, b)

            return carry

        lax.fori_loop(0, count, one, 0)

    def a_first(role):
        def body(i, b):
            fill(AX + 4 * role, i, b, 1, [])
            item(AX + 4 * role, i, to_pair).start()

        each(4, lambda i: a_row(role, i), body)

    def a_mid():
        def body(i, b):
            item(AX, i, to_pair).wait_recv()
            fill(AX + 8, i, b, 1, [AX + i])
            item(AX + 8, i, to_next).start()

        each(4, lambda i: a_row(2, i), body)

    def b_across(role):
        def body(i, b):
            fill(BZ + 2 * role, i, b, 0, [])
            item(BZ + 2 * role, i, partner).start()

        each(2, lambda i: b_row(role, i, 1 - zl), body)

    def b_first(role):
        def body(i, b):
            item(BZ + 2 * role, i, partner).wait_recv()
            fill(BX + 2 * role, i, b, 0, [BZ + 2 * role + i])
            item(BX + 2 * role, i, to_pair).start()

        each(2, lambda i: b_row(role, i, zl), body)

    def b_mid():
        def body(i, b):
            item(BZ + 4, i, partner).wait_recv()
            item(BX, i, to_pair).wait_recv()
            fill(BX + 4, i, b, 0, [BZ + 4 + i, BX + i])
            item(BX + 4, i, to_next).start()

        each(2, lambda i: b_row(2, i, zl), body)

    even = jnp.logical_not(odd)

    def a_home(z_from, z_to, i):
        slot = AZ + 2 * z_from + i
        to = (2 * x + z_to, swap_c)
        return remote(pout.at[AZ + 2 * z_to + i], pin.at[slot], p_send.at[AZ + 2 * z_to + i], p_recv.at[slot], to)

    def a_final(z_to, is_own):
        def body(i, b):
            item(AX + 4, 2 * z_to + i, to_pair).wait_recv()
            item(AX + 8, 2 * z_to + i, to_next).wait_recv()
            adds = [AX + 4 + 2 * z_to + i, AX + 8 + 2 * z_to + i]
            for k in range(8):
                rows = pl.ds(k * 64, 64)
                value = product(b, k, 1)
                for add in adds:
                    value = value + pin[add, rows, :].astype(jnp.float32)
                if is_own:
                    out_ref[pl.ds(i * 512 + k * 64, 64), 256:] = value
                pout[AZ + 2 * z_to + i, rows, :] = value.astype(jnp.bfloat16)

            @pl.when(odd)
            def _():
                a_home(zl, z_to, i).start()

            if not is_own:
                @pl.when(even)
                def _():
                    a_home(zl, z_to, i).start()

        each(2, lambda i: 4 * x + 2 * z_to + i, body)

    def b_home(i):
        return item(BS, i, (r, swap_c))

    def b_final():
        def body(i, b):
            item(BZ + 6, i, partner).wait_recv()
            item(BX + 2, i, to_pair).wait_recv()
            item(BX + 4, i, to_next).wait_recv()
            for k in range(8):
                rows = pl.ds(k * 64, 64)
                value = product(b, k, 0)
                for add in (BZ + 6 + i, BX + 2 + i, BX + 4 + i):
                    value = value + pin[add, rows, :].astype(jnp.float32)
                out_ref[pl.ds(i * 512 + k * 64, 64), :256] = value
                pout[BS + i, rows, :] = value.astype(jnp.bfloat16)

            @pl.when(odd)
            def _():
                b_home(i).start()

        each(2, lambda i: 4 * x + 2 * zl + i, body)

    b_across(0)
    a_first(0)
    b_across(1)
    a_first(1)
    b_across(2)
    b_across(3)
    b_first(0)
    a_mid()
    b_first(1)
    b_mid()
    a_final(1 - zl, False)
    a_final(zl, True)
    b_final()

    for i in range(2):
        b = 2 * r + i
        rows = pl.ds(i * 512, 512)

        @pl.when(b > c)
        def _():
            out_ref[rows, :] = jnp.zeros((512, 512), jnp.float32)

        @pl.when(jnp.logical_and(even, b <= c))
        def _():
            a_home(1 - zl, zl, i).wait_recv()
            out_ref[rows, 256:] = out_ref[rows, 256:] + pin[AZ + 2 * (1 - zl) + i].astype(jnp.float32)

        @pl.when(jnp.logical_and(odd, b <= c))
        def _():
            a_home(0, zl, i).wait_recv()
            a_home(1, zl, i).wait_recv()
            out_ref[rows, 256:] = pin[AZ + i].astype(jnp.float32) + pin[AZ + 2 + i].astype(jnp.float32)
            b_home(i).wait_recv()
            out_ref[rows, :256] = pin[BS + i].astype(jnp.float32)

    for copy in sent + col_copies:
        copy.wait_send()

    def left(count, row, copy, when=None):
        def one(i, carry):
            live = row(i) <= vc
            if when is not None:
                live = jnp.logical_and(live, when)

            @pl.when(live)
            def _():
                copy(i).wait_send()

            return carry

        lax.fori_loop(0, count, one, 0)

    for role in range(3):
        left(4, lambda i: a_row(role, i), lambda i: item(AX + 4 * role, i, to_pair))
        left(2, lambda i: b_row(role, i, zl), lambda i: item(BX + 2 * role, i, to_pair))
    for role in range(4):
        left(2, lambda i: b_row(role, i, 1 - zl), lambda i: item(BZ + 2 * role, i, partner))
    left(2, lambda i: 4 * x + 2 * (1 - zl) + i, lambda i: a_home(zl, 1 - zl, i))
    left(2, lambda i: 4 * x + 2 * zl + i, lambda i: a_home(zl, zl, i), odd)
    left(2, lambda i: 4 * x + 2 * zl + i, b_home, odd)


def local(densities, screened, q_table):
    block_len, pair_count, g_slice = densities.shape
    d = densities.reshape(block_len * pair_count, g_slice)
    bf = jnp.bfloat16
    dma = pltpu.SemaphoreType.DMA
    return pl.pallas_call(
        kernel,
        out_shape=jax.ShapeDtypeStruct((1024, 512), jnp.float32),
        in_specs=[
            pl.BlockSpec(memory_space=pl.ANY),
            pl.BlockSpec(memory_space=pl.ANY),
            pl.BlockSpec(memory_space=pltpu.SMEM),
        ],
        out_specs=pl.BlockSpec(memory_space=pltpu.VMEM),
        scratch_shapes=[
            pltpu.VMEM((16, 16, 256, 128), bf),
            pltpu.VMEM((16, 512, 256), bf),
            pltpu.VMEM((8, 512, 256), bf),
            pltpu.VMEM((512, 256), bf),
            pltpu.VMEM((16, 512, 256), bf),
            pltpu.VMEM((ITEMS, 512, 256), bf),
            pltpu.VMEM((ITEMS, 512, 256), bf),
            dma((4,)),
            dma((CHUNKS + 1, KINDS)),
            dma((CHUNKS + 1, KINDS)),
            dma((8,)),
            dma((8,)),
            dma((ITEMS,)),
            dma((ITEMS,)),
        ],
        compiler_params=pltpu.CompilerParams(
            collective_id=0, has_side_effects=True, vmem_limit_bytes=60 * 2**20
        ),
        cost_estimate=pl.CostEstimate(flops=10 * 10**9, bytes_accessed=4 * 2**20, transcendentals=0),
    )(d, screened, q_table)


def solution(mesh):
    return jax.shard_map(
        local,
        mesh=mesh,
        in_specs=(P("kc", None, "kr"), P(None, "kr", "kc"), P()),
        out_specs=P("kr", "kc"),
        check_vma=False,
    )
```

```python
import functools

import jax
import jax.numpy as jnp
from jax import lax
from jax.experimental import pallas as pl
from jax.experimental.pallas import tpu as pltpu
from jax.sharding import PartitionSpec as P

MESH = pl.DeviceIdType.MESH
NT = (((1,), (1,)), ((), ()))
CHUNKS = 4
AHEAD = 2
KINDS = 17
AX, AZ, BZ, BX, BS, ITEMS = 0, 12, 16, 24, 30, 32


def kernel(d_ref, w_ref, q_hbm, out_ref, q_ref, wb, drow, dcol, dtmp, yb, pout, pin,
           loc_sem, a_send, a_recv, d_send, d_recv, p_send, p_recv):
    r, c = lax.axis_index("kr"), lax.axis_index("kc")
    x, zl = r // 2, r % 2
    zh, y, core = c // 8, (c // 2) % 4, c % 2
    q_count = w_ref.shape[0]
    per = q_count // CHUNKS
    odd = core == 1
    vc = jnp.where(odd, 16 - c, c)
    swap_c = jnp.where(odd, 16 - c, c)

    def cid(zh_, y_, core_):
        return zh_ * 8 + y_ * 2 + core_

    yp, ym, y2, zo = (y + 1) % 4, (y + 3) % 4, (y + 2) % 4, 1 - zh
    up, down, across, sib = (r, cid(zh, yp, core)), (r, cid(zh, ym, core)), (r, cid(zo, y, core)), (r, cid(zh, y, 1 - core))

    partner = (2 * x + 1 - zl, c)

    def along(i):
        return 2 * ((x + i) % 4) + zl

    barrier = pltpu.get_barrier_semaphore()

    def greet(to):
        pl.semaphore_signal(barrier, inc=1, device_id=to, device_id_type=MESH)

    load_w = pltpu.make_async_copy(w_ref, wb.at[c], loc_sem.at[0])
    load_d = pltpu.make_async_copy(d_ref, drow.at[c], loc_sem.at[1])
    load_q = pltpu.make_async_copy(q_hbm, q_ref, loc_sem.at[4])
    load_w.start()
    load_d.start()
    load_q.start()
    for to in (up, down, across, sib, partner):
        greet(to)
    for i in range(1, 4):
        greet((along(i), c))

    @pl.when(odd)
    def _():
        greet((r, swap_c))
        greet((partner[0], swap_c))
        pl.semaphore_wait(barrier, 10)

    @pl.when(jnp.logical_not(odd))
    def _():
        pl.semaphore_wait(barrier, 8)

    load_d.wait()
    load_w.wait()

    def remote(src, dst, ssem, rsem, to):
        return pltpu.make_async_remote_copy(
            src_ref=src, dst_ref=dst, send_sem=ssem, recv_sem=rsem, device_id=to, device_id_type=MESH
        )

    swap_d = remote(drow.at[c], dtmp, d_send.at[7], d_recv.at[7], (r, swap_c))
    keep_d = pltpu.make_async_copy(drow.at[c], dtmp, loc_sem.at[2])

    @pl.when(odd)
    def _():
        swap_d.start()

    @pl.when(jnp.logical_not(odd))
    def _():
        keep_d.start()

    def part(s, who, half=None):
        if s < CHUNKS:
            if half is None:
                return wb.at[who, pl.ds(s * per, per)]
            return wb.at[who, pl.ds(s * per + half * (per // 2), per // 2)]
        if half is None:
            return drow.at[who]
        rows = drow.shape[1] // 2
        return drow.at[who, pl.ds(half * rows, rows)]

    sent = []

    def send(s, kind, who, to, recv_kind, half=None):
        ref = part(s, who, half)
        copy = remote(ref, ref, a_send.at[s, kind], a_recv.at[s, recv_kind], to)
        copy.start()
        if s < CHUNKS:
            sent.append(copy)

    def arrived(s, kind, who, half=None):
        ref = part(s, who, half)
        remote(ref, ref, a_send.at[s, kind], a_recv.at[s, kind], sib).wait_recv()

    c_ym, c_yp, c_y2 = cid(zh, ym, core), cid(zh, yp, core), cid(zh, y2, core)
    c_z, c_zym, c_zyp, c_zy2 = cid(zo, y, core), cid(zo, ym, core), cid(zo, yp, core), cid(zo, y2, core)
    blocks = [c, c_ym, c_yp, c_z, c_y2, c_zym, c_zyp, c_zy2]

    def own(s):
        send(s, 0, c, up, 0)
        send(s, 1, c, down, 1)
        send(s, 2, c, across, 2)
        send(s, 3, c, sib, 8)

    def relay_near(s):
        arrived(s, 0, c_ym)
        send(s, 4, c_ym, up, 3, 0)
        arrived(s, 1, c_yp)
        send(s, 6, c_yp, down, 4, 1)
        send(s, 5, c_ym, sib, 9)
        send(s, 7, c_yp, sib, 10)

    def relay_across(s):
        arrived(s, 2, c_z)
        send(s, 8, c_z, up, 5)
        send(s, 9, c_z, down, 6)
        send(s, 10, c_z, sib, 11)

    def relay_far(s):
        arrived(s, 3, c_y2, 0)
        arrived(s, 4, c_y2, 1)
        send(s, 11, c_y2, across, 7)
        send(s, 12, c_y2, sib, 12)

    def finish(s):
        arrived(s, 5, c_zym)
        send(s, 13, c_zym, sib, 13)
        arrived(s, 6, c_zyp)
        send(s, 14, c_zyp, sib, 14)
        arrived(s, 7, c_zy2)
        send(s, 15, c_zy2, sib, 15)
        for i, who in enumerate(blocks):
            arrived(s, 8 + i, who - core + (1 - core))

    rows_at = CHUNKS

    def near_out():
        send(rows_at, 0, c, up, 0)
        send(rows_at, 1, c, down, 1)
        send(rows_at, 3, c, sib, 8)

    def near_on():
        relay_near(rows_at)

    def near_end():
        arrived(rows_at, 3, c_y2, 0)
        arrived(rows_at, 4, c_y2, 1)
        send(rows_at, 12, c_y2, sib, 12)
        for i in (0, 1, 2, 4):
            arrived(rows_at, 8 + i, blocks[i] - core + (1 - core))

    def cross_out():
        relay_across(rows_at)

    def cross_on():
        arrived(rows_at, 5, c_zym)
        send(rows_at, 11, c_zym, up, 7, 0)
        arrived(rows_at, 6, c_zyp)
        send(rows_at, 16, c_zyp, down, 16, 1)
        send(rows_at, 13, c_zym, sib, 13)
        send(rows_at, 14, c_zyp, sib, 14)

    def cross_end():
        arrived(rows_at, 7, c_zy2, 0)
        arrived(rows_at, 16, c_zy2, 1)
        send(rows_at, 15, c_zy2, sib, 15)
        for i in (3, 5, 6, 7):
            arrived(rows_at, 8 + i, blocks[i] - core + (1 - core))

    def rows_step(near, cross, lower):
        pl.when(zh == (0 if lower else 1))(near)
        pl.when(zh == (1 if lower else 0))(cross)

    def screen(s):
        def one(i, carry):
            q = s * per + i
            lhs = jnp.concatenate([dcol[j] for j in range(8)], axis=1)
            rhs = jnp.concatenate([wb[j, q] for j in range(16)], axis=1)
            yb[q] = lax.dot_general(lhs, rhs, NT, preferred_element_type=jnp.float32).astype(jnp.bfloat16)
            return carry

        lax.fori_loop(0, per, one, 0)

    for s in range(AHEAD):
        own(s)

    @pl.when(odd)
    def _():
        swap_d.wait()

    @pl.when(jnp.logical_not(odd))
    def _():
        keep_d.wait()

    col_copies = []

    def col_send(i, src, who, to):
        copy = remote(src, dcol.at[who], d_send.at[i], d_recv.at[i], to)
        copy.start()
        col_copies.append(copy)

    def col_arrived(i, who):
        src = dcol.at[who]
        remote(src, src, d_send.at[i], d_recv.at[i], sib).wait_recv()

    col_send(0, dtmp, r, partner)
    for i in range(1, 4):
        col_send(i, dtmp, r, (along(i), c))
    col_own = pltpu.make_async_copy(dtmp, dcol.at[r], loc_sem.at[3])
    col_own.start()

    col_arrived(0, partner[0])
    for i in range(1, 4):
        col_send(3 + i, dcol.at[partner[0]], partner[0], (along(i), c))
    for s in range(CHUNKS):
        relay_near(s)
        if s + AHEAD < CHUNKS:
            own(s + AHEAD)
        elif s + AHEAD == CHUNKS:
            send(rows_at, 2, c, across, 2)
            pl.when(zh == 0)(near_out)
        if s >= 1:
            relay_far(s - 1)
    relay_across(0)
    relay_far(CHUNKS - 1)
    rows_step(near_on, cross_out, True)
    for s in range(1, CHUNKS):
        relay_across(s)
    col_own.wait()
    for i in range(1, 4):
        col_arrived(i, along(4 - i))
        col_arrived(3 + i, 2 * ((x + 4 - i) % 4) + 1 - zl)
    for s in range(CHUNKS - 1):
        finish(s)
        if s == 0:
            rows_step(lambda: None, cross_on, True)
        screen(s)
    rows_step(near_end, cross_end, True)
    finish(CHUNKS - 1)
    rows_step(near_out, cross_out, False)
    load_q.wait()
    screen(CHUNKS - 1)

    def product(b, k, half):
        rhs = jnp.concatenate(
            [yb[q_ref[b * 8 + k, vc * 8 + j], pl.ds(j * 64, 64), :] for j in range(4 * half, 4 * half + 4)], axis=0
        )
        lhs = drow[b, pl.ds(k * 64, 64), :]
        return lax.dot_general(lhs, rhs, NT, preferred_element_type=jnp.float32)

    step = 1 - 2 * (x % 2)
    x_far, x_pair, x_next = (x + 2) % 4, (x + 4 + step) % 4, (x + 4 - step) % 4
    to_pair, to_next = (2 * x_pair + zl, c), (2 * x_next + zl, c)
    dest = [x_far, x_pair, x_next, x]

    def a_row(role, i):
        to = dest[role] if isinstance(role, int) else jnp.where(role == 0, x_far, x_pair)
        return 4 * to + i

    def b_row(role, i, zl_):
        return 4 * dest[role] + 2 * zl_ + i

    def item(base, i, to):
        return remote(pout.at[base + i], pin.at[base + i], p_send.at[base + i], p_recv.at[base + i], to)

    def fill(base, i, b, half, adds):
        for k in range(8):
            rows = pl.ds(k * 64, 64)
            value = product(b, k, half)
            for add in adds:
                value = value + pin[add, rows, :].astype(jnp.float32)
            pout[base + i, rows, :] = value.astype(jnp.bfloat16)

    def each(count, row, body):
        def one(i, carry):
            b = row(i)

            @pl.when(b <= vc)
            def _():
                body(i, b)

            return carry

        lax.fori_loop(0, count, one, 0)

    def a_first(role):
        def body(i, b):
            fill(AX + 4 * role, i, b, 1, [])
            item(AX + 4 * role, i, to_pair).start()

        each(4, lambda i: a_row(role, i), body)

    def a_mid():
        def body(i, b):
            item(AX, i, to_pair).wait_recv()
            fill(AX + 8, i, b, 1, [AX + i])
            item(AX + 8, i, to_next).start()

        each(4, lambda i: a_row(2, i), body)

    zk = jnp.where(odd, 1 - zl, zl)

    def b_slot(to):
        return BZ + 2 * jnp.where(to == x_far, 0, jnp.where(to == x_pair, 1, jnp.where(to == x_next, 2, 3)))

    def b_across(to):
        base = b_slot(to)

        def body(i, b):
            fill(base, i, b, 0, [])
            item(base, i, partner).start()

        each(2, lambda i: 4 * to + 2 * (1 - zk) + i, body)

    def b_first(role):
        def body(i, b):
            item(BZ + 2 * role, i, partner).wait_recv()
            fill(BX + 2 * role, i, b, 0, [BZ + 2 * role + i])
            item(BX + 2 * role, i, to_pair).start()

        each(2, lambda i: b_row(role, i, zk), body)

    def b_mid():
        def body(i, b):
            item(BZ + 4, i, partner).wait_recv()
            item(BX, i, to_pair).wait_recv()
            fill(BX + 4, i, b, 0, [BZ + 4 + i, BX + i])
            item(BX + 4, i, to_next).start()

        each(2, lambda i: b_row(2, i, zk), body)

    even = jnp.logical_not(odd)

    def a_home(z_from, z_to, i):
        slot = AZ + 2 * z_from + i
        to = (2 * x + z_to, swap_c)
        return remote(pout.at[AZ + 2 * z_to + i], pin.at[slot], p_send.at[AZ + 2 * z_to + i], p_recv.at[slot], to)

    def a_final(z_to, is_own):
        def body(i, b):
            item(AX + 4, 2 * z_to + i, to_pair).wait_recv()
            item(AX + 8, 2 * z_to + i, to_next).wait_recv()
            adds = [AX + 4 + 2 * z_to + i, AX + 8 + 2 * z_to + i]
            for k in range(8):
                rows = pl.ds(k * 64, 64)
                value = product(b, k, 1)
                for add in adds:
                    value = value + pin[add, rows, :].astype(jnp.float32)
                if is_own:
                    out_ref[pl.ds(i * 512 + k * 64, 64), 256:] = value
                pout[AZ + 2 * z_to + i, rows, :] = value.astype(jnp.bfloat16)

            @pl.when(odd)
            def _():
                a_home(zl, z_to, i).start()

            if not is_own:
                @pl.when(even)
                def _():
                    a_home(zl, z_to, i).start()

        each(2, lambda i: 4 * x + 2 * z_to + i, body)

    def b_home(i):
        return item(BS, i, (2 * x + zk, swap_c))

    def b_final():
        def body(i, b):
            item(BZ + 6, i, partner).wait_recv()
            item(BX + 2, i, to_pair).wait_recv()
            item(BX + 4, i, to_next).wait_recv()
            for k in range(8):
                rows = pl.ds(k * 64, 64)
                value = product(b, k, 0)
                for add in (BZ + 6 + i, BX + 2 + i, BX + 4 + i):
                    value = value + pin[add, rows, :].astype(jnp.float32)
                out_ref[pl.ds(i * 512 + k * 64, 64), :256] = value
                pout[BS + i, rows, :] = value.astype(jnp.bfloat16)

            @pl.when(odd)
            def _():
                b_home(i).start()

        each(2, lambda i: 4 * x + 2 * zk + i, body)

    low_first = jnp.where(x >= 2, 0, 1)
    a_first(low_first)
    b_across(0)
    b_across(1)
    rows_step(near_on, cross_on, False)
    rows_step(near_end, cross_end, False)
    pl.when(x < 2)(lambda: a_first(0))
    b_across(2)
    b_across(3)
    a_mid()
    pl.when(x >= 2)(lambda: a_first(1))
    b_first(0)
    b_first(1)
    a_final(zl, True)
    a_final(1 - zl, False)
    b_mid()
    b_final()

    for i in range(2):
        b = 2 * r + i
        rows = pl.ds(i * 512, 512)

        @pl.when(b > c)
        def _():
            out_ref[rows, :] = jnp.zeros((512, 512), jnp.float32)

        @pl.when(jnp.logical_and(even, b <= c))
        def _():
            a_home(1 - zl, zl, i).wait_recv()
            out_ref[rows, 256:] = out_ref[rows, 256:] + pin[AZ + 2 * (1 - zl) + i].astype(jnp.float32)

        @pl.when(jnp.logical_and(odd, b <= c))
        def _():
            a_home(0, zl, i).wait_recv()
            a_home(1, zl, i).wait_recv()
            out_ref[rows, 256:] = pin[AZ + i].astype(jnp.float32) + pin[AZ + 2 + i].astype(jnp.float32)
            b_home(i).wait_recv()
            out_ref[rows, :256] = pin[BS + i].astype(jnp.float32)

    for copy in sent + col_copies:
        copy.wait_send()
    for kind in range(KINDS):
        ref = part(rows_at, c, 0 if kind in (4, 6, 11, 16) else None)
        remote(ref, ref, a_send.at[rows_at, kind], a_recv.at[rows_at, kind], sib).wait_send()

    def left(count, row, copy, when=None):
        def one(i, carry):
            live = row(i) <= vc
            if when is not None:
                live = jnp.logical_and(live, when)

            @pl.when(live)
            def _():
                copy(i).wait_send()

            return carry

        lax.fori_loop(0, count, one, 0)

    for role in range(3):
        left(4, lambda i: a_row(role, i), lambda i: item(AX + 4 * role, i, to_pair))
        left(2, lambda i: b_row(role, i, zk), lambda i: item(BX + 2 * role, i, to_pair))
    for role in range(4):
        left(2, lambda i: b_row(role, i, 1 - zk), lambda i: item(BZ + 2 * role, i, partner))
    left(2, lambda i: 4 * x + 2 * (1 - zl) + i, lambda i: a_home(zl, 1 - zl, i))
    left(2, lambda i: 4 * x + 2 * zl + i, lambda i: a_home(zl, zl, i), odd)
    left(2, lambda i: 4 * x + 2 * zk + i, b_home, odd)


def local(densities, screened, q_table):
    block_len, pair_count, g_slice = densities.shape
    d = densities.reshape(block_len * pair_count, g_slice)
    bf = jnp.bfloat16
    dma = pltpu.SemaphoreType.DMA
    return pl.pallas_call(
        kernel,
        out_shape=jax.ShapeDtypeStruct((1024, 512), jnp.float32),
        in_specs=[
            pl.BlockSpec(memory_space=pl.ANY),
            pl.BlockSpec(memory_space=pl.ANY),
            pl.BlockSpec(memory_space=pl.ANY),
        ],
        out_specs=pl.BlockSpec(memory_space=pltpu.VMEM),
        scratch_shapes=[
            pltpu.SMEM((128, 128), jnp.int32),
            pltpu.VMEM((16, 16, 256, 128), bf),
            pltpu.VMEM((16, 512, 256), bf),
            pltpu.VMEM((8, 512, 256), bf),
            pltpu.VMEM((512, 256), bf),
            pltpu.VMEM((16, 512, 256), bf),
            pltpu.VMEM((ITEMS, 512, 256), bf),
            pltpu.VMEM((ITEMS, 512, 256), bf),
            dma((5,)),
            dma((CHUNKS + 1, KINDS)),
            dma((CHUNKS + 1, KINDS)),
            dma((8,)),
            dma((8,)),
            dma((ITEMS,)),
            dma((ITEMS,)),
        ],
        compiler_params=pltpu.CompilerParams(
            collective_id=0, has_side_effects=True, vmem_limit_bytes=60 * 2**20
        ),
        cost_estimate=pl.CostEstimate(flops=10 * 10**9, bytes_accessed=4 * 2**20, transcendentals=0),
    )(d, screened, q_table)


def solution(mesh):
    return jax.shard_map(
        local,
        mesh=mesh,
        in_specs=(P("kc", None, "kr"), P(None, "kr", "kc"), P()),
        out_specs=P("kr", "kc"),
        check_vma=False,
    )
```

```python
import functools

import jax
import jax.numpy as jnp
from jax import lax
from jax.experimental import pallas as pl
from jax.experimental.pallas import tpu as pltpu
from jax.sharding import PartitionSpec as P

MESH = pl.DeviceIdType.MESH
NT = (((1,), (1,)), ((), ()))
CHUNKS = 4
AHEAD = 3
KINDS = 17
AX, AZ, BZ, BX, BS, ITEMS = 0, 12, 16, 24, 30, 32


def kernel(d_ref, w_ref, q_hbm, out_ref, q_ref, wb, drow, dcol, dtmp, yb, pout, pin,
           loc_sem, a_send, a_recv, d_send, d_recv, p_send, p_recv):
    r, c = lax.axis_index("kr"), lax.axis_index("kc")
    x, zl = r // 2, r % 2
    zh, y, core = c // 8, (c // 2) % 4, c % 2
    q_count = w_ref.shape[0]
    per = q_count // CHUNKS
    odd = core == 1
    vc = jnp.where(odd, 16 - c, c)
    swap_c = jnp.where(odd, 16 - c, c)

    def cid(zh_, y_, core_):
        return zh_ * 8 + y_ * 2 + core_

    yp, ym, y2, zo = (y + 1) % 4, (y + 3) % 4, (y + 2) % 4, 1 - zh
    up, down, across, sib = (r, cid(zh, yp, core)), (r, cid(zh, ym, core)), (r, cid(zo, y, core)), (r, cid(zh, y, 1 - core))

    partner = (2 * x + 1 - zl, c)

    def along(i):
        return 2 * ((x + i) % 4) + zl

    barrier = pltpu.get_barrier_semaphore()

    def greet(to):
        pl.semaphore_signal(barrier, inc=1, device_id=to, device_id_type=MESH)

    load_w = pltpu.make_async_copy(w_ref, wb.at[c], loc_sem.at[0])
    load_d = pltpu.make_async_copy(d_ref, drow.at[c], loc_sem.at[1])
    load_q = pltpu.make_async_copy(q_hbm, q_ref, loc_sem.at[4])
    load_w.start()
    load_d.start()
    load_q.start()
    for to in (up, down, across, sib, partner):
        greet(to)
    for i in range(1, 4):
        greet((along(i), c))

    @pl.when(odd)
    def _():
        greet((r, swap_c))
        greet((partner[0], swap_c))
        pl.semaphore_wait(barrier, 10)

    @pl.when(jnp.logical_not(odd))
    def _():
        pl.semaphore_wait(barrier, 8)

    load_d.wait()
    load_w.wait()

    def remote(src, dst, ssem, rsem, to):
        return pltpu.make_async_remote_copy(
            src_ref=src, dst_ref=dst, send_sem=ssem, recv_sem=rsem, device_id=to, device_id_type=MESH
        )

    swap_d = remote(drow.at[c], dtmp, d_send.at[7], d_recv.at[7], (r, swap_c))
    keep_d = pltpu.make_async_copy(drow.at[c], dtmp, loc_sem.at[2])

    @pl.when(odd)
    def _():
        swap_d.start()

    @pl.when(jnp.logical_not(odd))
    def _():
        keep_d.start()

    def part(s, who, half=None):
        if s < CHUNKS:
            if half is None:
                return wb.at[who, pl.ds(s * per, per)]
            return wb.at[who, pl.ds(s * per + half * (per // 2), per // 2)]
        if half is None:
            return drow.at[who]
        rows = drow.shape[1] // 2
        return drow.at[who, pl.ds(half * rows, rows)]

    sent = []

    def send(s, kind, who, to, recv_kind, half=None):
        ref = part(s, who, half)
        copy = remote(ref, ref, a_send.at[s, kind], a_recv.at[s, recv_kind], to)
        copy.start()
        if s < CHUNKS:
            sent.append(copy)

    def arrived(s, kind, who, half=None):
        ref = part(s, who, half)
        remote(ref, ref, a_send.at[s, kind], a_recv.at[s, kind], sib).wait_recv()

    c_ym, c_yp, c_y2 = cid(zh, ym, core), cid(zh, yp, core), cid(zh, y2, core)
    c_z, c_zym, c_zyp, c_zy2 = cid(zo, y, core), cid(zo, ym, core), cid(zo, yp, core), cid(zo, y2, core)
    blocks = [c, c_ym, c_yp, c_z, c_y2, c_zym, c_zyp, c_zy2]

    def own(s):
        send(s, 0, c, up, 0)
        send(s, 1, c, down, 1)
        send(s, 2, c, across, 2)
        send(s, 3, c, sib, 8)

    def relay_near(s):
        arrived(s, 0, c_ym)
        send(s, 4, c_ym, up, 3, 0)
        arrived(s, 1, c_yp)
        send(s, 6, c_yp, down, 4, 1)
        send(s, 5, c_ym, sib, 9)
        send(s, 7, c_yp, sib, 10)

    def relay_across(s):
        arrived(s, 2, c_z)
        send(s, 8, c_z, up, 5)
        send(s, 9, c_z, down, 6)
        send(s, 10, c_z, sib, 11)

    def relay_far(s):
        arrived(s, 3, c_y2, 0)
        arrived(s, 4, c_y2, 1)
        send(s, 11, c_y2, across, 7)
        send(s, 12, c_y2, sib, 12)

    def finish(s):
        arrived(s, 5, c_zym)
        send(s, 13, c_zym, sib, 13)
        arrived(s, 6, c_zyp)
        send(s, 14, c_zyp, sib, 14)
        arrived(s, 7, c_zy2)
        send(s, 15, c_zy2, sib, 15)
        for i, who in enumerate(blocks):
            arrived(s, 8 + i, who - core + (1 - core))

    rows_at = CHUNKS

    def near_out():
        send(rows_at, 0, c, up, 0)
        send(rows_at, 1, c, down, 1)
        send(rows_at, 3, c, sib, 8)

    def near_on():
        relay_near(rows_at)

    def near_end():
        arrived(rows_at, 3, c_y2, 0)
        arrived(rows_at, 4, c_y2, 1)
        send(rows_at, 12, c_y2, sib, 12)
        for i in (0, 1, 2, 4):
            arrived(rows_at, 8 + i, blocks[i] - core + (1 - core))

    def cross_out():
        relay_across(rows_at)

    def cross_on():
        arrived(rows_at, 5, c_zym)
        send(rows_at, 11, c_zym, up, 7, 0)
        arrived(rows_at, 6, c_zyp)
        send(rows_at, 16, c_zyp, down, 16, 1)
        send(rows_at, 13, c_zym, sib, 13)
        send(rows_at, 14, c_zyp, sib, 14)

    def cross_end():
        arrived(rows_at, 7, c_zy2, 0)
        arrived(rows_at, 16, c_zy2, 1)
        send(rows_at, 15, c_zy2, sib, 15)
        for i in (3, 5, 6, 7):
            arrived(rows_at, 8 + i, blocks[i] - core + (1 - core))

    def rows_step(near, cross, lower):
        pl.when(zh == (0 if lower else 1))(near)
        pl.when(zh == (1 if lower else 0))(cross)

    def screen(s):
        def one(i, carry):
            q = s * per + i
            lhs = jnp.concatenate([dcol[j] for j in range(8)], axis=1)
            rhs = jnp.concatenate([wb[j, q] for j in range(16)], axis=1)
            yb[q] = lax.dot_general(lhs, rhs, NT, preferred_element_type=jnp.float32).astype(jnp.bfloat16)
            return carry

        lax.fori_loop(0, per, one, 0)

    for s in range(AHEAD):
        own(s)

    col_copies = []

    def col_send(i, src, who, to):
        copy = remote(src, dcol.at[who], d_send.at[i], d_recv.at[i], to)
        copy.start()
        col_copies.append(copy)

    def col_arrived(i, who):
        src = dcol.at[who]
        remote(src, src, d_send.at[i], d_recv.at[i], sib).wait_recv()

    col_own = pltpu.make_async_copy(dtmp, dcol.at[r], loc_sem.at[3])

    def col_out():
        @pl.when(odd)
        def _():
            swap_d.wait()

        @pl.when(jnp.logical_not(odd))
        def _():
            keep_d.wait()

        col_send(0, dtmp, r, partner)
        for i in range(1, 4):
            col_send(i, dtmp, r, (along(i), c))
        col_own.start()

    def col_on():
        col_arrived(0, partner[0])
        for i in range(1, 4):
            col_send(3 + i, dcol.at[partner[0]], partner[0], (along(i), c))

    for s in range(CHUNKS):
        relay_near(s)
        if s == 0:
            col_out()
        if s == 1:
            col_on()
        if s + AHEAD < CHUNKS:
            own(s + AHEAD)
        elif s + AHEAD == CHUNKS:
            send(rows_at, 2, c, across, 2)
            pl.when(zh == 0)(near_out)
        if s >= 1:
            relay_far(s - 1)
    relay_across(0)
    relay_far(CHUNKS - 1)
    rows_step(near_on, cross_out, True)
    for s in range(1, CHUNKS):
        relay_across(s)
    col_own.wait()
    for i in range(1, 4):
        col_arrived(i, along(4 - i))
        col_arrived(3 + i, 2 * ((x + 4 - i) % 4) + 1 - zl)
    for s in range(CHUNKS - 1):
        finish(s)
        if s == 0:
            rows_step(lambda: None, cross_on, True)
        screen(s)
    rows_step(near_end, cross_end, True)
    finish(CHUNKS - 1)
    rows_step(near_out, cross_out, False)
    load_q.wait()
    screen(CHUNKS - 1)

    def product(b, k, half):
        rhs = jnp.concatenate(
            [yb[q_ref[b * 8 + k, vc * 8 + j], pl.ds(j * 64, 64), :] for j in range(4 * half, 4 * half + 4)], axis=0
        )
        lhs = drow[b, pl.ds(k * 64, 64), :]
        return lax.dot_general(lhs, rhs, NT, preferred_element_type=jnp.float32)

    step = 1 - 2 * (x % 2)
    x_far, x_pair, x_next = (x + 2) % 4, (x + 4 + step) % 4, (x + 4 - step) % 4
    to_pair, to_next = (2 * x_pair + zl, c), (2 * x_next + zl, c)
    dest = [x_far, x_pair, x_next, x]

    def a_row(role, i):
        to = dest[role] if isinstance(role, int) else jnp.where(role == 0, x_far, x_pair)
        return 4 * to + i

    def b_row(role, i, zl_):
        return 4 * dest[role] + 2 * zl_ + i

    def item(base, i, to):
        return remote(pout.at[base + i], pin.at[base + i], p_send.at[base + i], p_recv.at[base + i], to)

    def fill(base, i, b, half, adds):
        for k in range(8):
            rows = pl.ds(k * 64, 64)
            value = product(b, k, half)
            for add in adds:
                value = value + pin[add, rows, :].astype(jnp.float32)
            pout[base + i, rows, :] = value.astype(jnp.bfloat16)

    def each(count, row, body):
        def one(i, carry):
            b = row(i)

            @pl.when(b <= vc)
            def _():
                body(i, b)

            return carry

        lax.fori_loop(0, count, one, 0)

    def a_first(role):
        def body(i, b):
            fill(AX + 4 * role, i, b, 1, [])
            item(AX + 4 * role, i, to_pair).start()

        each(4, lambda i: a_row(role, i), body)

    def a_mid():
        def body(i, b):
            item(AX, i, to_pair).wait_recv()
            fill(AX + 8, i, b, 1, [AX + i])
            item(AX + 8, i, to_next).start()

        each(4, lambda i: a_row(2, i), body)

    zk = jnp.where(odd, 1 - zl, zl)

    def b_slot(to):
        return BZ + 2 * jnp.where(to == x_far, 0, jnp.where(to == x_pair, 1, jnp.where(to == x_next, 2, 3)))

    def b_across(to):
        base = b_slot(to)

        def body(i, b):
            fill(base, i, b, 0, [])
            item(base, i, partner).start()

        each(2, lambda i: 4 * to + 2 * (1 - zk) + i, body)

    def b_first(role):
        def body(i, b):
            item(BZ + 2 * role, i, partner).wait_recv()
            fill(BX + 2 * role, i, b, 0, [BZ + 2 * role + i])
            item(BX + 2 * role, i, to_pair).start()

        each(2, lambda i: b_row(role, i, zk), body)

    def b_mid():
        def body(i, b):
            item(BZ + 4, i, partner).wait_recv()
            item(BX, i, to_pair).wait_recv()
            fill(BX + 4, i, b, 0, [BZ + 4 + i, BX + i])
            item(BX + 4, i, to_next).start()

        each(2, lambda i: b_row(2, i, zk), body)

    even = jnp.logical_not(odd)

    def a_home(z_from, z_to, i):
        slot = AZ + 2 * z_from + i
        to = (2 * x + z_to, swap_c)
        return remote(pout.at[AZ + 2 * z_to + i], pin.at[slot], p_send.at[AZ + 2 * z_to + i], p_recv.at[slot], to)

    def a_final(z_to, is_own):
        def body(i, b):
            item(AX + 4, 2 * z_to + i, to_pair).wait_recv()
            item(AX + 8, 2 * z_to + i, to_next).wait_recv()
            adds = [AX + 4 + 2 * z_to + i, AX + 8 + 2 * z_to + i]
            for k in range(8):
                rows = pl.ds(k * 64, 64)
                value = product(b, k, 1)
                for add in adds:
                    value = value + pin[add, rows, :].astype(jnp.float32)
                if is_own:
                    out_ref[pl.ds(i * 512 + k * 64, 64), 256:] = value
                pout[AZ + 2 * z_to + i, rows, :] = value.astype(jnp.bfloat16)

            @pl.when(odd)
            def _():
                a_home(zl, z_to, i).start()

            if not is_own:
                @pl.when(even)
                def _():
                    a_home(zl, z_to, i).start()

        each(2, lambda i: 4 * x + 2 * z_to + i, body)

    def b_home(i):
        return item(BS, i, (2 * x + zk, swap_c))

    def b_final():
        def body(i, b):
            item(BZ + 6, i, partner).wait_recv()
            item(BX + 2, i, to_pair).wait_recv()
            item(BX + 4, i, to_next).wait_recv()
            for k in range(8):
                rows = pl.ds(k * 64, 64)
                value = product(b, k, 0)
                for add in (BZ + 6 + i, BX + 2 + i, BX + 4 + i):
                    value = value + pin[add, rows, :].astype(jnp.float32)
                out_ref[pl.ds(i * 512 + k * 64, 64), :256] = value
                pout[BS + i, rows, :] = value.astype(jnp.bfloat16)

            @pl.when(odd)
            def _():
                b_home(i).start()

        each(2, lambda i: 4 * x + 2 * zk + i, body)

    low_first = jnp.where(x >= 2, 0, 1)
    a_first(low_first)
    b_across(0)
    b_across(1)
    rows_step(near_on, cross_on, False)
    rows_step(near_end, cross_end, False)
    pl.when(x < 2)(lambda: a_first(0))
    b_across(2)
    b_across(3)
    a_mid()
    pl.when(x >= 2)(lambda: a_first(1))
    b_first(0)
    b_first(1)
    a_final(zl, True)
    a_final(1 - zl, False)
    b_mid()
    b_final()

    for i in range(2):
        b = 2 * r + i
        rows = pl.ds(i * 512, 512)

        @pl.when(b > c)
        def _():
            out_ref[rows, :] = jnp.zeros((512, 512), jnp.float32)

        @pl.when(jnp.logical_and(even, b <= c))
        def _():
            a_home(1 - zl, zl, i).wait_recv()
            out_ref[rows, 256:] = out_ref[rows, 256:] + pin[AZ + 2 * (1 - zl) + i].astype(jnp.float32)

        @pl.when(jnp.logical_and(odd, b <= c))
        def _():
            a_home(0, zl, i).wait_recv()
            a_home(1, zl, i).wait_recv()
            out_ref[rows, 256:] = pin[AZ + i].astype(jnp.float32) + pin[AZ + 2 + i].astype(jnp.float32)
            b_home(i).wait_recv()
            out_ref[rows, :256] = pin[BS + i].astype(jnp.float32)

    for copy in sent + col_copies:
        copy.wait_send()
    for kind in range(KINDS):
        ref = part(rows_at, c, 0 if kind in (4, 6, 11, 16) else None)
        remote(ref, ref, a_send.at[rows_at, kind], a_recv.at[rows_at, kind], sib).wait_send()

    def left(count, row, copy, when=None):
        def one(i, carry):
            live = row(i) <= vc
            if when is not None:
                live = jnp.logical_and(live, when)

            @pl.when(live)
            def _():
                copy(i).wait_send()

            return carry

        lax.fori_loop(0, count, one, 0)

    for role in range(3):
        left(4, lambda i: a_row(role, i), lambda i: item(AX + 4 * role, i, to_pair))
        left(2, lambda i: b_row(role, i, zk), lambda i: item(BX + 2 * role, i, to_pair))
    for role in range(4):
        left(2, lambda i: b_row(role, i, 1 - zk), lambda i: item(BZ + 2 * role, i, partner))
    left(2, lambda i: 4 * x + 2 * (1 - zl) + i, lambda i: a_home(zl, 1 - zl, i))
    left(2, lambda i: 4 * x + 2 * zl + i, lambda i: a_home(zl, zl, i), odd)
    left(2, lambda i: 4 * x + 2 * zk + i, b_home, odd)


def local(densities, screened, q_table):
    block_len, pair_count, g_slice = densities.shape
    d = densities.reshape(block_len * pair_count, g_slice)
    bf = jnp.bfloat16
    dma = pltpu.SemaphoreType.DMA
    return pl.pallas_call(
        kernel,
        out_shape=pltpu.VMEM((1024, 512), jnp.float32),
        in_specs=[
            pl.BlockSpec(memory_space=pl.ANY),
            pl.BlockSpec(memory_space=pl.ANY),
            pl.BlockSpec(memory_space=pl.ANY),
        ],
        out_specs=pl.BlockSpec(memory_space=pltpu.VMEM),
        scratch_shapes=[
            pltpu.SMEM((128, 128), jnp.int32),
            pltpu.VMEM((16, 16, 256, 128), bf),
            pltpu.VMEM((16, 512, 256), bf),
            pltpu.VMEM((8, 512, 256), bf),
            pltpu.VMEM((512, 256), bf),
            pltpu.VMEM((16, 512, 256), bf),
            pltpu.VMEM((ITEMS, 512, 256), bf),
            pltpu.VMEM((ITEMS, 512, 256), bf),
            dma((5,)),
            dma((CHUNKS + 1, KINDS)),
            dma((CHUNKS + 1, KINDS)),
            dma((8,)),
            dma((8,)),
            dma((ITEMS,)),
            dma((ITEMS,)),
        ],
        compiler_params=pltpu.CompilerParams(
            collective_id=0, has_side_effects=True, vmem_limit_bytes=61 * 2**20
        ),
        cost_estimate=pl.CostEstimate(flops=10 * 10**9, bytes_accessed=4 * 2**20, transcendentals=0),
    )(d, screened, q_table)


def solution(mesh):
    return jax.shard_map(
        local,
        mesh=mesh,
        in_specs=(P("kc", None, "kr"), P(None, "kr", "kc"), P()),
        out_specs=P("kr", "kc"),
        check_vma=False,
    )
```

```python
import functools

import jax
import jax.numpy as jnp
from jax import lax
from jax.experimental import pallas as pl
from jax.experimental.pallas import tpu as pltpu
from jax.sharding import PartitionSpec as P

MESH = pl.DeviceIdType.MESH
NT = (((1,), (1,)), ((), ()))
SIZES = (4, 4, 4, 4)
STARTS = (0, 4, 8, 12)
CHUNKS = len(SIZES)
AHEAD = 3
KINDS = 17
AX, AZ, BZ, BX, BS, ITEMS = 0, 12, 16, 24, 30, 32


def kernel(d_ref, w_ref, q_hbm, out_ref, q_ref, wb, drow, dcol, dtmp, yb, pout, pin, acc,
           loc_sem, a_send, a_recv, d_send, d_recv, p_send, p_recv):
    r, c = lax.axis_index("kr"), lax.axis_index("kc")
    x, zl = r // 2, r % 2
    zh, y, core = c // 8, (c // 2) % 4, c % 2
    odd = core == 1
    vc = jnp.where(odd, 16 - c, c)
    swap_c = jnp.where(odd, 16 - c, c)

    def cid(zh_, y_, core_):
        return zh_ * 8 + y_ * 2 + core_

    yp, ym, y2, zo = (y + 1) % 4, (y + 3) % 4, (y + 2) % 4, 1 - zh
    up, down, across, sib = (r, cid(zh, yp, core)), (r, cid(zh, ym, core)), (r, cid(zo, y, core)), (r, cid(zh, y, 1 - core))

    partner = (2 * x + 1 - zl, c)

    def along(i):
        return 2 * ((x + i) % 4) + zl

    barrier = pltpu.get_barrier_semaphore()

    def greet(to):
        pl.semaphore_signal(barrier, inc=1, device_id=to, device_id_type=MESH)

    load_w = pltpu.make_async_copy(w_ref, wb.at[c], loc_sem.at[0])
    load_d = pltpu.make_async_copy(d_ref, drow.at[c], loc_sem.at[1])
    load_q = pltpu.make_async_copy(q_hbm, q_ref, loc_sem.at[4])
    load_w.start()
    load_d.start()
    load_q.start()
    for to in (up, down, across, sib, partner):
        greet(to)
    for i in range(1, 4):
        greet((along(i), c))

    @pl.when(odd)
    def _():
        greet((r, swap_c))
        greet((partner[0], swap_c))
        pl.semaphore_wait(barrier, 10)

    @pl.when(jnp.logical_not(odd))
    def _():
        pl.semaphore_wait(barrier, 8)

    load_d.wait()
    load_w.wait()

    def remote(src, dst, ssem, rsem, to):
        return pltpu.make_async_remote_copy(
            src_ref=src, dst_ref=dst, send_sem=ssem, recv_sem=rsem, device_id=to, device_id_type=MESH
        )

    swap_d = remote(drow.at[c], dtmp, d_send.at[7], d_recv.at[7], (r, swap_c))
    keep_d = pltpu.make_async_copy(drow.at[c], dtmp, loc_sem.at[2])

    @pl.when(odd)
    def _():
        swap_d.start()

    @pl.when(jnp.logical_not(odd))
    def _():
        keep_d.start()

    def part(s, who, half=None):
        if s < CHUNKS:
            if half is None:
                return wb.at[who, pl.ds(STARTS[s], SIZES[s])]
            return wb.at[who, pl.ds(STARTS[s] + half * (SIZES[s] // 2), SIZES[s] // 2)]
        if half is None:
            return drow.at[who]
        rows = drow.shape[1] // 2
        return drow.at[who, pl.ds(half * rows, rows)]

    sent = []

    def send(s, kind, who, to, recv_kind, half=None):
        ref = part(s, who, half)
        copy = remote(ref, ref, a_send.at[s, kind], a_recv.at[s, recv_kind], to)
        copy.start()
        if s < CHUNKS:
            sent.append(copy)

    def arrived(s, kind, who, half=None):
        ref = part(s, who, half)
        remote(ref, ref, a_send.at[s, kind], a_recv.at[s, kind], sib).wait_recv()

    c_ym, c_yp, c_y2 = cid(zh, ym, core), cid(zh, yp, core), cid(zh, y2, core)
    c_z, c_zym, c_zyp, c_zy2 = cid(zo, y, core), cid(zo, ym, core), cid(zo, yp, core), cid(zo, y2, core)
    blocks = [c, c_ym, c_yp, c_z, c_y2, c_zym, c_zyp, c_zy2]

    def own(s):
        send(s, 0, c, up, 0)
        send(s, 1, c, down, 1)
        send(s, 2, c, across, 2)
        send(s, 3, c, sib, 8)

    def relay_near(s):
        arrived(s, 0, c_ym)
        send(s, 4, c_ym, up, 3, 0)
        arrived(s, 1, c_yp)
        send(s, 6, c_yp, down, 4, 1)
        send(s, 5, c_ym, sib, 9)
        send(s, 7, c_yp, sib, 10)

    def relay_across(s):
        arrived(s, 2, c_z)
        send(s, 8, c_z, up, 5)
        send(s, 9, c_z, down, 6)
        send(s, 10, c_z, sib, 11)

    def relay_far(s):
        arrived(s, 3, c_y2, 0)
        arrived(s, 4, c_y2, 1)
        send(s, 11, c_y2, across, 7)
        send(s, 12, c_y2, sib, 12)

    def finish(s, between=None):
        arrived(s, 5, c_zym)
        send(s, 13, c_zym, sib, 13)
        arrived(s, 6, c_zyp)
        send(s, 14, c_zyp, sib, 14)
        if between is not None:
            between()
        arrived(s, 7, c_zy2)
        send(s, 15, c_zy2, sib, 15)
        for i, who in enumerate(blocks):
            if not (between is not None and i < 5):
                arrived(s, 8 + i, who - core + (1 - core))

    rows_at = CHUNKS

    def near_out():
        send(rows_at, 0, c, up, 0)
        send(rows_at, 1, c, down, 1)
        send(rows_at, 3, c, sib, 8)

    def near_on():
        relay_near(rows_at)

    def near_end():
        arrived(rows_at, 3, c_y2, 0)
        arrived(rows_at, 4, c_y2, 1)
        send(rows_at, 12, c_y2, sib, 12)
        for i in (0, 1, 2, 4):
            arrived(rows_at, 8 + i, blocks[i] - core + (1 - core))

    def cross_out():
        relay_across(rows_at)

    def cross_on():
        arrived(rows_at, 5, c_zym)
        send(rows_at, 11, c_zym, up, 7, 0)
        arrived(rows_at, 6, c_zyp)
        send(rows_at, 16, c_zyp, down, 16, 1)
        send(rows_at, 13, c_zym, sib, 13)
        send(rows_at, 14, c_zyp, sib, 14)

    def cross_end():
        arrived(rows_at, 7, c_zy2, 0)
        arrived(rows_at, 16, c_zy2, 1)
        send(rows_at, 15, c_zy2, sib, 15)
        for i in (3, 5, 6, 7):
            arrived(rows_at, 8 + i, blocks[i] - core + (1 - core))

    def rows_step(near, cross, lower):
        pl.when(zh == (0 if lower else 1))(near)
        pl.when(zh == (1 if lower else 0))(cross)

    def screen(s):
        def one(i, carry):
            q = STARTS[s] + i
            lhs = jnp.concatenate([dcol[j] for j in range(8)], axis=1)
            rhs = jnp.concatenate([wb[j, q] for j in range(16)], axis=1)
            yb[q] = lax.dot_general(lhs, rhs, NT, preferred_element_type=jnp.float32).astype(jnp.bfloat16)
            return carry

        lax.fori_loop(0, SIZES[s], one, 0)

    def screen_part(s, chips, first):
        def one(i, carry):
            q = STARTS[s] + i
            lhs = jnp.concatenate([dcol[j] for j in chips], axis=1)
            rhs = jnp.concatenate([wb[2 * j + k, q] for j in chips for k in range(2)], axis=1)
            value = lax.dot_general(lhs, rhs, NT, preferred_element_type=jnp.float32)
            if first:
                acc[i] = value
            else:
                yb[q] = (acc[i] + value).astype(jnp.bfloat16)
            return carry

        lax.fori_loop(0, SIZES[s], one, 0)

    for s in range(AHEAD):
        own(s)

    col_copies = []

    def col_send(i, src, who, to):
        copy = remote(src, dcol.at[who], d_send.at[i], d_recv.at[i], to)
        copy.start()
        col_copies.append(copy)

    def col_arrived(i, who):
        src = dcol.at[who]
        remote(src, src, d_send.at[i], d_recv.at[i], sib).wait_recv()

    col_own = pltpu.make_async_copy(dtmp, dcol.at[r], loc_sem.at[3])

    def col_out():
        @pl.when(odd)
        def _():
            swap_d.wait()

        @pl.when(jnp.logical_not(odd))
        def _():
            keep_d.wait()

        col_send(0, dtmp, r, partner)
        for i in range(1, 4):
            col_send(i, dtmp, r, (along(i), c))
        col_own.start()

    def col_on():
        col_arrived(0, partner[0])
        for i in range(1, 4):
            col_send(3 + i, dcol.at[partner[0]], partner[0], (along(i), c))

    relay_near(0)
    col_out()
    own(3)
    relay_near(1)
    col_on()
    send(rows_at, 2, c, across, 2)
    relay_far(0)
    relay_near(2)
    relay_far(1)
    relay_near(3)
    relay_far(2)
    relay_across(0)
    relay_far(3)
    relay_across(1)
    relay_across(2)
    relay_across(3)
    rows_step(near_out, cross_out, True)
    col_own.wait()
    for i in range(1, 4):
        col_arrived(i, along(4 - i))
        col_arrived(3 + i, 2 * ((x + 4 - i) % 4) + 1 - zl)
    for s in range(CHUNKS - 1):
        finish(s)
        screen(s)
    for i, who in enumerate(blocks[:5]):
        arrived(CHUNKS - 1, 8 + i, who - core + (1 - core))
    chips = [who // 2 for who in blocks]
    screen_part(CHUNKS - 1, chips[:5], True)
    finish(CHUNKS - 1, lambda: rows_step(near_on, cross_on, True))
    load_q.wait()
    screen_part(CHUNKS - 1, chips[5:], False)
    rows_step(near_out, cross_out, False)
    rows_step(near_end, cross_end, True)

    def product(b, k, half):
        rhs = jnp.concatenate(
            [yb[q_ref[b * 8 + k, vc * 8 + j], pl.ds(j * 64, 64), :] for j in range(4 * half, 4 * half + 4)], axis=0
        )
        lhs = drow[b, pl.ds(k * 64, 64), :]
        return lax.dot_general(lhs, rhs, NT, preferred_element_type=jnp.float32)

    step = 1 - 2 * (x % 2)
    x_far, x_pair, x_next = (x + 2) % 4, (x + 4 + step) % 4, (x + 4 - step) % 4
    to_pair, to_next = (2 * x_pair + zl, c), (2 * x_next + zl, c)
    dest = [x_far, x_pair, x_next, x]

    def a_row(role, i):
        to = dest[role] if isinstance(role, int) else jnp.where(role == 0, x_far, x_pair)
        return 4 * to + i

    def b_row(role, i, zl_):
        to = dest[role] if isinstance(role, int) else jnp.where(role == 0, x_far, x_pair)
        return 4 * to + 2 * zl_ + i

    def item(base, i, to):
        return remote(pout.at[base + i], pin.at[base + i], p_send.at[base + i], p_recv.at[base + i], to)

    def fill(base, i, b, half, adds):
        for k in range(8):
            rows = pl.ds(k * 64, 64)
            value = product(b, k, half)
            for add in adds:
                value = value + pin[add, rows, :].astype(jnp.float32)
            pout[base + i, rows, :] = value.astype(jnp.bfloat16)

    def each(count, row, body):
        def one(i, carry):
            b = row(i)

            @pl.when(b <= vc)
            def _():
                body(i, b)

            return carry

        lax.fori_loop(0, count, one, 0)

    def a_first(role):
        def body(i, b):
            fill(AX + 4 * role, i, b, 1, [])
            item(AX + 4 * role, i, to_pair).start()

        each(4, lambda i: a_row(role, i), body)

    def a_mid():
        def body(i, b):
            item(AX, i, to_pair).wait_recv()
            fill(AX + 8, i, b, 1, [AX + i])
            item(AX + 8, i, to_next).start()

        each(4, lambda i: a_row(2, i), body)

    zk = jnp.where(odd, 1 - zl, zl)

    def b_slot(to):
        return BZ + 2 * jnp.where(to == x_far, 0, jnp.where(to == x_pair, 1, jnp.where(to == x_next, 2, 3)))

    def b_across(to):
        base = b_slot(to)

        def body(i, b):
            fill(base, i, b, 0, [])
            item(base, i, partner).start()

        each(2, lambda i: 4 * to + 2 * (1 - zk) + i, body)

    def b_first(role):
        def body(i, b):
            item(BZ + 2 * role, i, partner).wait_recv()
            fill(BX + 2 * role, i, b, 0, [BZ + 2 * role + i])
            item(BX + 2 * role, i, to_pair).start()

        each(2, lambda i: b_row(role, i, zk), body)

    def b_mid():
        def body(i, b):
            item(BZ + 4, i, partner).wait_recv()
            item(BX, i, to_pair).wait_recv()
            fill(BX + 4, i, b, 0, [BZ + 4 + i, BX + i])
            item(BX + 4, i, to_next).start()

        each(2, lambda i: b_row(2, i, zk), body)

    even = jnp.logical_not(odd)

    def a_home(z_from, z_to, i):
        slot = AZ + 2 * z_from + i
        to = (2 * x + z_to, swap_c)
        return remote(pout.at[AZ + 2 * z_to + i], pin.at[slot], p_send.at[AZ + 2 * z_to + i], p_recv.at[slot], to)

    def a_final(z_to, is_own):
        def body(i, b):
            item(AX + 4, 2 * z_to + i, to_pair).wait_recv()
            item(AX + 8, 2 * z_to + i, to_next).wait_recv()
            adds = [AX + 4 + 2 * z_to + i, AX + 8 + 2 * z_to + i]
            for k in range(8):
                rows = pl.ds(k * 64, 64)
                value = product(b, k, 1)
                for add in adds:
                    value = value + pin[add, rows, :].astype(jnp.float32)
                if is_own:
                    out_ref[pl.ds(i * 512 + k * 64, 64), 256:] = value
                pout[AZ + 2 * z_to + i, rows, :] = value.astype(jnp.bfloat16)

            @pl.when(odd)
            def _():
                a_home(zl, z_to, i).start()

            if not is_own:
                @pl.when(even)
                def _():
                    a_home(zl, z_to, i).start()

        each(2, lambda i: 4 * x + 2 * z_to + i, body)

    def b_home(i):
        return item(BS, i, (2 * x + zk, swap_c))

    def b_final():
        def body(i, b):
            item(BZ + 6, i, partner).wait_recv()
            item(BX + 2, i, to_pair).wait_recv()
            item(BX + 4, i, to_next).wait_recv()
            for k in range(8):
                rows = pl.ds(k * 64, 64)
                value = product(b, k, 0)
                for add in (BZ + 6 + i, BX + 2 + i, BX + 4 + i):
                    value = value + pin[add, rows, :].astype(jnp.float32)
                out_ref[pl.ds(i * 512 + k * 64, 64), :256] = value
                pout[BS + i, rows, :] = value.astype(jnp.bfloat16)

            @pl.when(odd)
            def _():
                b_home(i).start()

        each(2, lambda i: 4 * x + 2 * zk + i, body)

    def left(count, row, copy, when=None):
        def one(i, carry):
            live = row(i) <= vc
            if when is not None:
                live = jnp.logical_and(live, when)

            @pl.when(live)
            def _():
                copy(i).wait_send()

            return carry

        lax.fori_loop(0, count, one, 0)

    def gather_left():
        for copy in sent + col_copies:
            copy.wait_send()

    def rows_left():
        for kind in range(KINDS):
            ref = part(rows_at, c, 0 if kind in (4, 6, 11, 16) else None)
            remote(ref, ref, a_send.at[rows_at, kind], a_recv.at[rows_at, kind], sib).wait_send()

    def first_left():
        for role in range(3):
            left(4, lambda i: a_row(role, i), lambda i: item(AX + 4 * role, i, to_pair))
        for role in range(4):
            left(2, lambda i: b_row(role, i, 1 - zk), lambda i: item(BZ + 2 * role, i, partner))

    low_first = jnp.where(x >= 2, 0, 1)
    a_first(low_first)
    b_across(0)
    b_across(1)
    rows_step(near_on, cross_on, False)
    gather_left()
    rows_step(near_end, cross_end, False)
    pl.when(x < 2)(lambda: a_first(0))
    b_across(2)
    b_across(3)
    pl.when(x >= 2)(lambda: a_first(1))
    a_mid()
    b_first(low_first)
    b_first(1 - low_first)
    a_final(zl, True)
    a_final(1 - zl, False)
    rows_left()
    b_mid()
    first_left()
    b_final()

    for i in range(2):
        b = 2 * r + i
        rows = pl.ds(i * 512, 512)

        @pl.when(b > c)
        def _():
            out_ref[rows, :] = jnp.zeros((512, 512), jnp.float32)

        @pl.when(jnp.logical_and(even, b <= c))
        def _():
            a_home(1 - zl, zl, i).wait_recv()
            out_ref[rows, 256:] = out_ref[rows, 256:] + pin[AZ + 2 * (1 - zl) + i].astype(jnp.float32)

        @pl.when(jnp.logical_and(odd, b <= c))
        def _():
            a_home(0, zl, i).wait_recv()
            a_home(1, zl, i).wait_recv()
            out_ref[rows, 256:] = pin[AZ + i].astype(jnp.float32) + pin[AZ + 2 + i].astype(jnp.float32)
            b_home(i).wait_recv()
            out_ref[rows, :256] = pin[BS + i].astype(jnp.float32)

    for role in range(3):
        left(2, lambda i: b_row(role, i, zk), lambda i: item(BX + 2 * role, i, to_pair))
    left(2, lambda i: 4 * x + 2 * (1 - zl) + i, lambda i: a_home(zl, 1 - zl, i))
    left(2, lambda i: 4 * x + 2 * zl + i, lambda i: a_home(zl, zl, i), odd)
    left(2, lambda i: 4 * x + 2 * zk + i, b_home, odd)


def local(densities, screened, q_table):
    block_len, pair_count, g_slice = densities.shape
    d = densities.reshape(block_len * pair_count, g_slice)
    bf = jnp.bfloat16
    dma = pltpu.SemaphoreType.DMA
    return pl.pallas_call(
        kernel,
        out_shape=pltpu.VMEM((1024, 512), jnp.float32),
        in_specs=[
            pl.BlockSpec(memory_space=pl.ANY),
            pl.BlockSpec(memory_space=pl.ANY),
            pl.BlockSpec(memory_space=pl.ANY),
        ],
        out_specs=pl.BlockSpec(memory_space=pltpu.VMEM),
        scratch_shapes=[
            pltpu.SMEM((128, 128), jnp.int32),
            pltpu.VMEM((16, 16, 256, 128), bf),
            pltpu.VMEM((16, 512, 256), bf),
            pltpu.VMEM((8, 512, 256), bf),
            pltpu.VMEM((512, 256), bf),
            pltpu.VMEM((16, 512, 256), bf),
            pltpu.VMEM((ITEMS, 512, 256), bf),
            pltpu.VMEM((ITEMS, 512, 256), bf),
            pltpu.VMEM((SIZES[-1], 512, 256), jnp.float32),
            dma((5,)),
            dma((CHUNKS + 1, KINDS)),
            dma((CHUNKS + 1, KINDS)),
            dma((8,)),
            dma((8,)),
            dma((ITEMS,)),
            dma((ITEMS,)),
        ],
        compiler_params=pltpu.CompilerParams(
            collective_id=0, has_side_effects=True, vmem_limit_bytes=61 * 2**20
        ),
        cost_estimate=pl.CostEstimate(flops=10 * 10**9, bytes_accessed=4 * 2**20, transcendentals=0),
    )(d, screened, q_table)


def solution(mesh):
    return jax.shard_map(
        local,
        mesh=mesh,
        in_specs=(P("kc", None, "kr"), P(None, "kr", "kc"), P()),
        out_specs=P("kr", "kc"),
        check_vma=False,
    )
```

```python
import functools

import jax
import jax.numpy as jnp
from jax import lax
from jax.experimental import pallas as pl
from jax.experimental.pallas import tpu as pltpu
from jax.sharding import PartitionSpec as P

MESH = pl.DeviceIdType.MESH
NT = (((1,), (1,)), ((), ()))
SIZES = (4, 4, 4, 4)
STARTS = (0, 4, 8, 12)
CHUNKS = len(SIZES)
AHEAD = 3
KINDS = 17
AX, AZ, BZ, BX, BS, ITEMS = 0, 12, 16, 24, 30, 32


def kernel(d_ref, w_ref, q_hbm, out_ref, q_ref, wb, drow, dcol, dtmp, yb, pout, pin, acc,
           loc_sem, a_send, a_recv, d_send, d_recv, p_send, p_recv):
    r, c = lax.axis_index("kr"), lax.axis_index("kc")
    x, zl = r // 2, r % 2
    zh, y, core = c // 8, (c // 2) % 4, c % 2
    odd = core == 1
    vc = jnp.where(odd, 16 - c, c)
    swap_c = jnp.where(odd, 16 - c, c)

    def cid(zh_, y_, core_):
        return zh_ * 8 + y_ * 2 + core_

    yp, ym, y2, zo = (y + 1) % 4, (y + 3) % 4, (y + 2) % 4, 1 - zh
    up, down, across, sib = (r, cid(zh, yp, core)), (r, cid(zh, ym, core)), (r, cid(zo, y, core)), (r, cid(zh, y, 1 - core))

    partner = (2 * x + 1 - zl, c)

    def along(i):
        return 2 * ((x + i) % 4) + zl

    barrier = pltpu.get_barrier_semaphore()

    def greet(to):
        pl.semaphore_signal(barrier, inc=1, device_id=to, device_id_type=MESH)

    load_w = pltpu.make_async_copy(w_ref, wb.at[c], loc_sem.at[0])
    load_d = pltpu.make_async_copy(d_ref, drow.at[c], loc_sem.at[1])
    load_q = pltpu.make_async_copy(q_hbm, q_ref, loc_sem.at[4])
    load_w.start()
    load_d.start()
    load_q.start()
    for to in (up, down, across, sib, partner):
        greet(to)
    for i in range(1, 4):
        greet((along(i), c))

    @pl.when(odd)
    def _():
        greet((r, swap_c))
        greet((partner[0], swap_c))
        pl.semaphore_wait(barrier, 10)

    @pl.when(jnp.logical_not(odd))
    def _():
        pl.semaphore_wait(barrier, 8)

    load_d.wait()
    load_w.wait()

    def remote(src, dst, ssem, rsem, to):
        return pltpu.make_async_remote_copy(
            src_ref=src, dst_ref=dst, send_sem=ssem, recv_sem=rsem, device_id=to, device_id_type=MESH
        )

    swap_d = remote(drow.at[c], dtmp, d_send.at[7], d_recv.at[7], (r, swap_c))
    keep_d = pltpu.make_async_copy(drow.at[c], dtmp, loc_sem.at[2])

    @pl.when(odd)
    def _():
        swap_d.start()

    @pl.when(jnp.logical_not(odd))
    def _():
        keep_d.start()

    def part(s, who, half=None):
        if s < CHUNKS:
            if half is None:
                return wb.at[who, pl.ds(STARTS[s], SIZES[s])]
            return wb.at[who, pl.ds(STARTS[s] + half * (SIZES[s] // 2), SIZES[s] // 2)]
        if half is None:
            return drow.at[who]
        rows = drow.shape[1] // 2
        return drow.at[who, pl.ds(half * rows, rows)]

    sent = []

    def send(s, kind, who, to, recv_kind, half=None):
        ref = part(s, who, half)
        copy = remote(ref, ref, a_send.at[s, kind], a_recv.at[s, recv_kind], to)
        copy.start()
        if s < CHUNKS:
            sent.append(copy)

    def arrived(s, kind, who, half=None):
        ref = part(s, who, half)
        remote(ref, ref, a_send.at[s, kind], a_recv.at[s, kind], sib).wait_recv()

    c_ym, c_yp, c_y2 = cid(zh, ym, core), cid(zh, yp, core), cid(zh, y2, core)
    c_z, c_zym, c_zyp, c_zy2 = cid(zo, y, core), cid(zo, ym, core), cid(zo, yp, core), cid(zo, y2, core)
    blocks = [c, c_ym, c_yp, c_z, c_y2, c_zym, c_zyp, c_zy2]

    def own(s):
        send(s, 0, c, up, 0)
        send(s, 1, c, down, 1)
        send(s, 2, c, across, 2)
        send(s, 3, c, sib, 8)

    def relay_near(s):
        arrived(s, 0, c_ym)
        send(s, 4, c_ym, up, 3, 0)
        arrived(s, 1, c_yp)
        send(s, 6, c_yp, down, 4, 1)
        send(s, 5, c_ym, sib, 9)
        send(s, 7, c_yp, sib, 10)

    def relay_across(s):
        arrived(s, 2, c_z)
        send(s, 8, c_z, up, 5)
        send(s, 9, c_z, down, 6)

    def relay_far(s):
        arrived(s, 3, c_y2, 0)
        arrived(s, 4, c_y2, 1)
        send(s, 11, c_y2, across, 7)
        send(s, 12, c_y2, sib, 12)

    def finish(s, between=None):
        arrived(s, 5, c_zym)
        send(s, 13, c_zym, sib, 13)
        arrived(s, 6, c_zyp)
        send(s, 14, c_zyp, sib, 14)
        if between is not None:
            between()
        arrived(s, 7, c_zy2)
        send(s, 15, c_zy2, sib, 15)
        for i, who in enumerate(blocks):
            if not (between is not None and i < 5):
                arrived(s, 8 + i, who - core + (1 - core))

    rows_at = CHUNKS

    def near_out():
        send(rows_at, 0, c, up, 0)
        send(rows_at, 1, c, down, 1)
        send(rows_at, 3, c, sib, 8)

    def near_on():
        relay_near(rows_at)

    def near_end():
        arrived(rows_at, 3, c_y2, 0)
        arrived(rows_at, 4, c_y2, 1)
        send(rows_at, 12, c_y2, sib, 12)
        for i in (0, 1, 2, 4):
            arrived(rows_at, 8 + i, blocks[i] - core + (1 - core))

    def cross_out():
        relay_across(rows_at)
        send(rows_at, 10, c_z, sib, 11)

    def cross_on():
        arrived(rows_at, 5, c_zym)
        send(rows_at, 11, c_zym, up, 7, 0)
        arrived(rows_at, 6, c_zyp)
        send(rows_at, 16, c_zyp, down, 16, 1)
        send(rows_at, 13, c_zym, sib, 13)
        send(rows_at, 14, c_zyp, sib, 14)

    def cross_end():
        arrived(rows_at, 7, c_zy2, 0)
        arrived(rows_at, 16, c_zy2, 1)
        send(rows_at, 15, c_zy2, sib, 15)
        for i in (3, 5, 6, 7):
            arrived(rows_at, 8 + i, blocks[i] - core + (1 - core))

    def rows_step(near, cross, lower):
        pl.when(zh == (0 if lower else 1))(near)
        pl.when(zh == (1 if lower else 0))(cross)

    def screen(s):
        def one(i, carry):
            q = STARTS[s] + i
            lhs = jnp.concatenate([dcol[j] for j in range(8)], axis=1)
            rhs = jnp.concatenate([wb[j, q] for j in range(16)], axis=1)
            yb[q] = lax.dot_general(lhs, rhs, NT, preferred_element_type=jnp.float32).astype(jnp.bfloat16)
            return carry

        lax.fori_loop(0, SIZES[s], one, 0)

    def screen_part(s, chips, first):
        def one(i, carry):
            q = STARTS[s] + i
            lhs = jnp.concatenate([dcol[j] for j in chips], axis=1)
            rhs = jnp.concatenate([wb[2 * j + k, q] for j in chips for k in range(2)], axis=1)
            value = lax.dot_general(lhs, rhs, NT, preferred_element_type=jnp.float32)
            if first:
                acc[i] = value
            else:
                yb[q] = (acc[i] + value).astype(jnp.bfloat16)
            return carry

        lax.fori_loop(0, SIZES[s], one, 0)

    for s in range(AHEAD):
        own(s)

    col_copies = []

    def col_send(i, src, who, to):
        copy = remote(src, dcol.at[who], d_send.at[i], d_recv.at[i], to)
        copy.start()
        col_copies.append(copy)

    def col_arrived(i, who):
        src = dcol.at[who]
        remote(src, src, d_send.at[i], d_recv.at[i], sib).wait_recv()

    col_own = pltpu.make_async_copy(dtmp, dcol.at[r], loc_sem.at[3])

    def col_out():
        @pl.when(odd)
        def _():
            swap_d.wait()

        @pl.when(jnp.logical_not(odd))
        def _():
            keep_d.wait()

        col_send(0, dtmp, r, partner)
        for i in range(1, 4):
            col_send(i, dtmp, r, (along(i), c))
        col_own.start()

    def col_on():
        col_arrived(0, partner[0])
        for i in range(1, 4):
            col_send(3 + i, dcol.at[partner[0]], partner[0], (along(i), c))

    relay_near(0)
    col_out()
    own(3)
    relay_near(1)
    col_on()
    send(rows_at, 2, c, across, 2)
    relay_far(0)
    relay_near(2)
    relay_far(1)
    relay_near(3)
    relay_far(2)
    relay_across(0)
    relay_far(3)
    relay_across(1)
    relay_across(2)
    relay_across(3)
    rows_step(near_out, cross_out, True)
    for s in range(CHUNKS):
        send(s, 10, c_z, sib, 11)
    col_own.wait()
    for i in range(1, 4):
        col_arrived(i, along(4 - i))
        col_arrived(3 + i, 2 * ((x + 4 - i) % 4) + 1 - zl)
    for s in range(CHUNKS - 1):
        finish(s)
        screen(s)
    for i, who in enumerate(blocks[:5]):
        arrived(CHUNKS - 1, 8 + i, who - core + (1 - core))
    chips = [who // 2 for who in blocks]
    screen_part(CHUNKS - 1, chips[:5], True)
    finish(CHUNKS - 1, lambda: (rows_step(near_on, cross_on, True), rows_step(near_out, cross_out, False)))
    load_q.wait()
    screen_part(CHUNKS - 1, chips[5:], False)
    rows_step(near_end, cross_end, True)

    def product(b, k, half):
        rhs = jnp.concatenate(
            [yb[q_ref[b * 8 + k, vc * 8 + j], pl.ds(j * 64, 64), :] for j in range(4 * half, 4 * half + 4)], axis=0
        )
        lhs = drow[b, pl.ds(k * 64, 64), :]
        return lax.dot_general(lhs, rhs, NT, preferred_element_type=jnp.float32)

    step = 1 - 2 * (x % 2)
    x_far, x_pair, x_next = (x + 2) % 4, (x + 4 + step) % 4, (x + 4 - step) % 4
    to_pair, to_next = (2 * x_pair + zl, c), (2 * x_next + zl, c)
    dest = [x_far, x_pair, x_next, x]

    def a_row(role, i):
        to = dest[role] if isinstance(role, int) else jnp.where(role == 0, x_far, x_pair)
        return 4 * to + i

    def b_row(role, i, zl_):
        to = dest[role] if isinstance(role, int) else jnp.where(role == 0, x_far, x_pair)
        return 4 * to + 2 * zl_ + i

    def item(base, i, to):
        return remote(pout.at[base + i], pin.at[base + i], p_send.at[base + i], p_recv.at[base + i], to)

    def fill(base, i, b, half, adds):
        for k in range(8):
            rows = pl.ds(k * 64, 64)
            value = product(b, k, half)
            for add in adds:
                value = value + pin[add, rows, :].astype(jnp.float32)
            pout[base + i, rows, :] = value.astype(jnp.bfloat16)

    def each(count, row, body):
        def one(i, carry):
            b = row(i)

            @pl.when(b <= vc)
            def _():
                body(i, b)

            return carry

        lax.fori_loop(0, count, one, 0)

    def a_first(role):
        def body(i, b):
            fill(AX + 4 * role, i, b, 1, [])
            item(AX + 4 * role, i, to_pair).start()

        each(4, lambda i: a_row(role, i), body)

    def a_mid():
        def body(i, b):
            item(AX, i, to_pair).wait_recv()
            fill(AX + 8, i, b, 1, [AX + i])
            item(AX + 8, i, to_next).start()

        each(4, lambda i: a_row(2, i), body)

    zk = jnp.where(odd, 1 - zl, zl)

    def b_slot(to):
        return BZ + 2 * jnp.where(to == x_far, 0, jnp.where(to == x_pair, 1, jnp.where(to == x_next, 2, 3)))

    def b_across(to):
        base = b_slot(to)

        def body(i, b):
            fill(base, i, b, 0, [])
            item(base, i, partner).start()

        each(2, lambda i: 4 * to + 2 * (1 - zk) + i, body)

    def b_first(role):
        def body(i, b):
            item(BZ + 2 * role, i, partner).wait_recv()
            fill(BX + 2 * role, i, b, 0, [BZ + 2 * role + i])
            item(BX + 2 * role, i, to_pair).start()

        each(2, lambda i: b_row(role, i, zk), body)

    def b_mid():
        def body(i, b):
            item(BZ + 4, i, partner).wait_recv()
            item(BX, i, to_pair).wait_recv()
            fill(BX + 4, i, b, 0, [BZ + 4 + i, BX + i])
            item(BX + 4, i, to_next).start()

        each(2, lambda i: b_row(2, i, zk), body)

    even = jnp.logical_not(odd)

    def a_home(z_from, z_to, i):
        slot = AZ + 2 * z_from + i
        to = (2 * x + z_to, swap_c)
        return remote(pout.at[AZ + 2 * z_to + i], pin.at[slot], p_send.at[AZ + 2 * z_to + i], p_recv.at[slot], to)

    def a_final(z_to, is_own):
        def body(i, b):
            item(AX + 4, 2 * z_to + i, to_pair).wait_recv()
            item(AX + 8, 2 * z_to + i, to_next).wait_recv()
            adds = [AX + 4 + 2 * z_to + i, AX + 8 + 2 * z_to + i]
            for k in range(8):
                rows = pl.ds(k * 64, 64)
                value = product(b, k, 1)
                for add in adds:
                    value = value + pin[add, rows, :].astype(jnp.float32)
                if is_own:
                    out_ref[pl.ds(i * 512 + k * 64, 64), 256:] = value
                pout[AZ + 2 * z_to + i, rows, :] = value.astype(jnp.bfloat16)

            @pl.when(odd)
            def _():
                a_home(zl, z_to, i).start()

            if not is_own:
                @pl.when(even)
                def _():
                    a_home(zl, z_to, i).start()

        each(2, lambda i: 4 * x + 2 * z_to + i, body)

    def b_home(i):
        return item(BS, i, (2 * x + zk, swap_c))

    def b_final():
        def body(i, b):
            item(BZ + 6, i, partner).wait_recv()
            item(BX + 2, i, to_pair).wait_recv()
            item(BX + 4, i, to_next).wait_recv()
            for k in range(8):
                rows = pl.ds(k * 64, 64)
                value = product(b, k, 0)
                for add in (BZ + 6 + i, BX + 2 + i, BX + 4 + i):
                    value = value + pin[add, rows, :].astype(jnp.float32)
                out_ref[pl.ds(i * 512 + k * 64, 64), :256] = value
                pout[BS + i, rows, :] = value.astype(jnp.bfloat16)

            @pl.when(odd)
            def _():
                b_home(i).start()

        each(2, lambda i: 4 * x + 2 * zk + i, body)

    def left(count, row, copy, when=None):
        def one(i, carry):
            live = row(i) <= vc
            if when is not None:
                live = jnp.logical_and(live, when)

            @pl.when(live)
            def _():
                copy(i).wait_send()

            return carry

        lax.fori_loop(0, count, one, 0)

    def gather_left():
        for copy in sent + col_copies:
            copy.wait_send()

    def rows_left():
        for kind in range(KINDS):
            ref = part(rows_at, c, 0 if kind in (4, 6, 11, 16) else None)
            remote(ref, ref, a_send.at[rows_at, kind], a_recv.at[rows_at, kind], sib).wait_send()

    def first_left():
        for role in range(3):
            left(4, lambda i: a_row(role, i), lambda i: item(AX + 4 * role, i, to_pair))
        for role in range(4):
            left(2, lambda i: b_row(role, i, 1 - zk), lambda i: item(BZ + 2 * role, i, partner))

    low_first = jnp.where(x >= 2, 0, 1)
    def even_order_0():
        b_across(0)
        b_across(1)
        a_first(low_first)

    def odd_order_0():
        a_first(low_first)
        b_across(0)
        b_across(1)

    pl.when(even)(even_order_0)
    pl.when(odd)(odd_order_0)
    rows_step(near_on, cross_on, False)
    gather_left()
    rows_step(near_end, cross_end, False)
    pl.when(x < 2)(lambda: a_first(0))
    b_across(2)
    b_across(3)
    pl.when(x >= 2)(lambda: a_first(1))
    a_mid()
    b_first(low_first)
    b_first(1 - low_first)
    a_final(zl, True)
    a_final(1 - zl, False)
    rows_left()
    b_mid()
    first_left()
    b_final()

    for i in range(2):
        b = 2 * r + i
        rows = pl.ds(i * 512, 512)

        @pl.when(b > c)
        def _():
            out_ref[rows, :] = jnp.zeros((512, 512), jnp.float32)

        @pl.when(jnp.logical_and(even, b <= c))
        def _():
            a_home(1 - zl, zl, i).wait_recv()
            out_ref[rows, 256:] = out_ref[rows, 256:] + pin[AZ + 2 * (1 - zl) + i].astype(jnp.float32)

        @pl.when(jnp.logical_and(odd, b <= c))
        def _():
            a_home(0, zl, i).wait_recv()
            a_home(1, zl, i).wait_recv()
            out_ref[rows, 256:] = pin[AZ + i].astype(jnp.float32) + pin[AZ + 2 + i].astype(jnp.float32)
            b_home(i).wait_recv()
            out_ref[rows, :256] = pin[BS + i].astype(jnp.float32)

    for role in range(3):
        left(2, lambda i: b_row(role, i, zk), lambda i: item(BX + 2 * role, i, to_pair))
    left(2, lambda i: 4 * x + 2 * (1 - zl) + i, lambda i: a_home(zl, 1 - zl, i))
    left(2, lambda i: 4 * x + 2 * zl + i, lambda i: a_home(zl, zl, i), odd)
    left(2, lambda i: 4 * x + 2 * zk + i, b_home, odd)


def local(densities, screened, q_table):
    block_len, pair_count, g_slice = densities.shape
    d = densities.reshape(block_len * pair_count, g_slice)
    bf = jnp.bfloat16
    dma = pltpu.SemaphoreType.DMA
    return pl.pallas_call(
        kernel,
        out_shape=pltpu.VMEM((1024, 512), jnp.float32),
        in_specs=[
            pl.BlockSpec(memory_space=pl.ANY),
            pl.BlockSpec(memory_space=pl.ANY),
            pl.BlockSpec(memory_space=pl.ANY),
        ],
        out_specs=pl.BlockSpec(memory_space=pltpu.VMEM),
        scratch_shapes=[
            pltpu.SMEM((128, 128), jnp.int32),
            pltpu.VMEM((16, 16, 256, 128), bf),
            pltpu.VMEM((16, 512, 256), bf),
            pltpu.VMEM((8, 512, 256), bf),
            pltpu.VMEM((512, 256), bf),
            pltpu.VMEM((16, 512, 256), bf),
            pltpu.VMEM((ITEMS, 512, 256), bf),
            pltpu.VMEM((ITEMS, 512, 256), bf),
            pltpu.VMEM((SIZES[-1], 512, 256), jnp.float32),
            dma((5,)),
            dma((CHUNKS + 1, KINDS)),
            dma((CHUNKS + 1, KINDS)),
            dma((8,)),
            dma((8,)),
            dma((ITEMS,)),
            dma((ITEMS,)),
        ],
        compiler_params=pltpu.CompilerParams(
            collective_id=0, has_side_effects=True, vmem_limit_bytes=61 * 2**20
        ),
        cost_estimate=pl.CostEstimate(flops=10 * 10**9, bytes_accessed=4 * 2**20, transcendentals=0),
    )(d, screened, q_table)


def solution(mesh):
    return jax.shard_map(
        local,
        mesh=mesh,
        in_specs=(P("kc", None, "kr"), P(None, "kr", "kc"), P()),
        out_specs=P("kr", "kc"),
        check_vma=False,
    )
```

```python
import functools

import jax
import jax.numpy as jnp
from jax import lax
from jax.experimental import pallas as pl
from jax.experimental.pallas import tpu as pltpu
from jax.sharding import PartitionSpec as P

MESH = pl.DeviceIdType.MESH
NT = (((1,), (1,)), ((), ()))
SIZES = (4, 4, 4, 4)
STARTS = (0, 4, 8, 12)
CHUNKS = len(SIZES)
AHEAD = 3
KINDS = 17
AX, AZ, BZ, BX, BS, ITEMS = 0, 12, 16, 24, 30, 32


def kernel(d_ref, w_ref, q_hbm, out_ref, q_ref, wb, drow, dcol, dtmp, yb, pout, pin, acc,
           loc_sem, a_send, a_recv, d_send, d_recv, p_send, p_recv):
    r, c = lax.axis_index("kr"), lax.axis_index("kc")
    x, zl = r // 2, r % 2
    zh, y, core = c // 8, (c // 2) % 4, c % 2
    odd = core == 1
    vc = jnp.where(odd, 16 - c, c)
    swap_c = jnp.where(odd, 16 - c, c)

    def cid(zh_, y_, core_):
        return zh_ * 8 + y_ * 2 + core_

    yp, ym, y2, zo = (y + 1) % 4, (y + 3) % 4, (y + 2) % 4, 1 - zh
    up, down, across, sib = (r, cid(zh, yp, core)), (r, cid(zh, ym, core)), (r, cid(zo, y, core)), (r, cid(zh, y, 1 - core))

    partner = (2 * x + 1 - zl, c)

    def along(i):
        return 2 * ((x + i) % 4) + zl

    barrier = pltpu.get_barrier_semaphore()

    def greet(to):
        pl.semaphore_signal(barrier, inc=1, device_id=to, device_id_type=MESH)

    load_w = pltpu.make_async_copy(w_ref, wb.at[c], loc_sem.at[0])
    load_d = pltpu.make_async_copy(d_ref, drow.at[c], loc_sem.at[1])
    load_q = pltpu.make_async_copy(q_hbm, q_ref, loc_sem.at[4])
    load_w.start()
    load_d.start()
    load_q.start()
    for to in (up, down, across, sib, partner):
        greet(to)
    for i in range(1, 4):
        greet((along(i), c))

    @pl.when(odd)
    def _():
        greet((r, swap_c))
        greet((partner[0], swap_c))
        pl.semaphore_wait(barrier, 10)

    @pl.when(jnp.logical_not(odd))
    def _():
        pl.semaphore_wait(barrier, 8)

    load_d.wait()
    load_w.wait()

    def remote(src, dst, ssem, rsem, to):
        return pltpu.make_async_remote_copy(
            src_ref=src, dst_ref=dst, send_sem=ssem, recv_sem=rsem, device_id=to, device_id_type=MESH
        )

    swap_d = remote(drow.at[c], dtmp, d_send.at[7], d_recv.at[7], (r, swap_c))
    keep_d = pltpu.make_async_copy(drow.at[c], dtmp, loc_sem.at[2])

    @pl.when(odd)
    def _():
        swap_d.start()

    @pl.when(jnp.logical_not(odd))
    def _():
        keep_d.start()

    def part(s, who, half=None):
        if s < CHUNKS:
            if half is None:
                return wb.at[who, pl.ds(STARTS[s], SIZES[s])]
            return wb.at[who, pl.ds(STARTS[s] + half * (SIZES[s] // 2), SIZES[s] // 2)]
        if half is None:
            return drow.at[who]
        rows = drow.shape[1] // 2
        return drow.at[who, pl.ds(half * rows, rows)]

    sent = []

    def send(s, kind, who, to, recv_kind, half=None):
        ref = part(s, who, half)
        copy = remote(ref, ref, a_send.at[s, kind], a_recv.at[s, recv_kind], to)
        copy.start()
        if s < CHUNKS:
            sent.append(copy)

    def arrived(s, kind, who, half=None):
        ref = part(s, who, half)
        remote(ref, ref, a_send.at[s, kind], a_recv.at[s, kind], sib).wait_recv()

    c_ym, c_yp, c_y2 = cid(zh, ym, core), cid(zh, yp, core), cid(zh, y2, core)
    c_z, c_zym, c_zyp, c_zy2 = cid(zo, y, core), cid(zo, ym, core), cid(zo, yp, core), cid(zo, y2, core)
    blocks = [c, c_ym, c_yp, c_z, c_y2, c_zym, c_zyp, c_zy2]

    def own(s):
        send(s, 0, c, up, 0)
        send(s, 1, c, down, 1)
        send(s, 2, c, across, 2)
        send(s, 3, c, sib, 8)

    def relay_near(s):
        arrived(s, 0, c_ym)
        send(s, 4, c_ym, up, 3, 0)
        arrived(s, 1, c_yp)
        send(s, 6, c_yp, down, 4, 1)
        send(s, 5, c_ym, sib, 9)
        send(s, 7, c_yp, sib, 10)

    def relay_across(s):
        arrived(s, 2, c_z)
        send(s, 8, c_z, up, 5)
        send(s, 9, c_z, down, 6)
        send(s, 10, c_z, sib, 11)

    def relay_far(s):
        arrived(s, 3, c_y2, 0)
        arrived(s, 4, c_y2, 1)
        send(s, 11, c_y2, across, 7)
        send(s, 12, c_y2, sib, 12)

    def finish(s, between=None):
        arrived(s, 5, c_zym)
        send(s, 13, c_zym, sib, 13)
        arrived(s, 6, c_zyp)
        send(s, 14, c_zyp, sib, 14)
        if between is not None:
            between()
        arrived(s, 7, c_zy2)
        send(s, 15, c_zy2, sib, 15)
        for i, who in enumerate(blocks):
            if not (between is not None and i < 5):
                arrived(s, 8 + i, who - core + (1 - core))

    rows_at = CHUNKS

    def near_out():
        send(rows_at, 0, c, up, 0)
        send(rows_at, 1, c, down, 1)
        send(rows_at, 3, c, sib, 8)

    def near_on():
        relay_near(rows_at)

    def near_end():
        arrived(rows_at, 3, c_y2, 0)
        arrived(rows_at, 4, c_y2, 1)
        send(rows_at, 12, c_y2, sib, 12)
        for i in (0, 1, 2, 4):
            arrived(rows_at, 8 + i, blocks[i] - core + (1 - core))

    def cross_out():
        relay_across(rows_at)

    def cross_on():
        arrived(rows_at, 5, c_zym)
        send(rows_at, 11, c_zym, up, 7, 0)
        arrived(rows_at, 6, c_zyp)
        send(rows_at, 16, c_zyp, down, 16, 1)
        send(rows_at, 13, c_zym, sib, 13)
        send(rows_at, 14, c_zyp, sib, 14)

    def cross_end():
        arrived(rows_at, 7, c_zy2, 0)
        arrived(rows_at, 16, c_zy2, 1)
        send(rows_at, 15, c_zy2, sib, 15)
        for i in (3, 5, 6, 7):
            arrived(rows_at, 8 + i, blocks[i] - core + (1 - core))

    def rows_step(near, cross, lower):
        pl.when(zh == (0 if lower else 1))(near)
        pl.when(zh == (1 if lower else 0))(cross)

    def screen(s):
        def one(i, carry):
            q = STARTS[s] + i
            lhs = jnp.concatenate([dcol[j] for j in range(8)], axis=1)
            rhs = jnp.concatenate([wb[j, q] for j in range(16)], axis=1)
            yb[q] = lax.dot_general(lhs, rhs, NT, preferred_element_type=jnp.float32).astype(jnp.bfloat16)
            return carry

        lax.fori_loop(0, SIZES[s], one, 0)

    def screen_part(s, chips, first):
        def one(i, carry):
            q = STARTS[s] + i
            lhs = jnp.concatenate([dcol[j] for j in chips], axis=1)
            rhs = jnp.concatenate([wb[2 * j + k, q] for j in chips for k in range(2)], axis=1)
            value = lax.dot_general(lhs, rhs, NT, preferred_element_type=jnp.float32)
            if first:
                acc[i] = value
            else:
                yb[q] = (acc[i] + value).astype(jnp.bfloat16)
            return carry

        lax.fori_loop(0, SIZES[s], one, 0)

    for s in range(AHEAD):
        own(s)

    col_copies = []

    def col_send(i, src, who, to):
        copy = remote(src, dcol.at[who], d_send.at[i], d_recv.at[i], to)
        copy.start()
        col_copies.append(copy)

    def col_arrived(i, who):
        src = dcol.at[who]
        remote(src, src, d_send.at[i], d_recv.at[i], sib).wait_recv()

    col_own = pltpu.make_async_copy(dtmp, dcol.at[r], loc_sem.at[3])

    def col_out():
        @pl.when(odd)
        def _():
            swap_d.wait()

        @pl.when(jnp.logical_not(odd))
        def _():
            keep_d.wait()

        col_send(0, dtmp, r, partner)
        for i in range(1, 4):
            col_send(i, dtmp, r, (along(i), c))
        col_own.start()

    def col_on():
        col_arrived(0, partner[0])
        for i in range(1, 4):
            col_send(3 + i, dcol.at[partner[0]], partner[0], (along(i), c))

    relay_near(0)
    col_out()
    own(3)
    relay_near(1)
    col_on()
    send(rows_at, 2, c, across, 2)
    relay_far(0)
    relay_near(2)
    relay_far(1)
    relay_near(3)
    relay_far(2)
    relay_across(0)
    relay_far(3)
    relay_across(1)
    relay_across(2)
    relay_across(3)
    rows_step(near_out, cross_out, True)
    col_own.wait()
    for i in range(1, 4):
        col_arrived(i, along(4 - i))
        col_arrived(3 + i, 2 * ((x + 4 - i) % 4) + 1 - zl)
    for s in range(CHUNKS - 1):
        finish(s)
        screen(s)
    for i, who in enumerate(blocks[:5]):
        arrived(CHUNKS - 1, 8 + i, who - core + (1 - core))
    chips = [who // 2 for who in blocks]
    screen_part(CHUNKS - 1, chips[:5], True)
    finish(CHUNKS - 1, lambda: rows_step(near_on, cross_on, True))
    load_q.wait()
    screen_part(CHUNKS - 1, chips[5:], False)
    rows_step(near_out, cross_out, False)
    rows_step(near_end, cross_end, True)

    def product(b, k, half):
        rhs = jnp.concatenate(
            [yb[q_ref[b * 8 + k, vc * 8 + j], pl.ds(j * 64, 64), :] for j in range(4 * half, 4 * half + 4)], axis=0
        )
        lhs = drow[b, pl.ds(k * 64, 64), :]
        return lax.dot_general(lhs, rhs, NT, preferred_element_type=jnp.float32)

    step = 1 - 2 * (x % 2)
    x_far, x_pair, x_next = (x + 2) % 4, (x + 4 + step) % 4, (x + 4 - step) % 4
    to_pair, to_next = (2 * x_pair + zl, c), (2 * x_next + zl, c)
    dest = [x_far, x_pair, x_next, x]

    def a_row(role, i):
        to = dest[role] if isinstance(role, int) else jnp.where(role == 0, x_far, x_pair)
        return 4 * to + i

    def b_row(role, i, zl_):
        to = dest[role] if isinstance(role, int) else jnp.where(role == 0, x_far, x_pair)
        return 4 * to + 2 * zl_ + i

    def item(base, i, to):
        return remote(pout.at[base + i], pin.at[base + i], p_send.at[base + i], p_recv.at[base + i], to)

    def fill(base, i, b, half, adds):
        for k in range(8):
            rows = pl.ds(k * 64, 64)
            value = product(b, k, half)
            for add in adds:
                value = value + pin[add, rows, :].astype(jnp.float32)
            pout[base + i, rows, :] = value.astype(jnp.bfloat16)

    def each(count, row, body):
        def one(i, carry):
            b = row(i)

            @pl.when(b <= vc)
            def _():
                body(i, b)

            return carry

        lax.fori_loop(0, count, one, 0)

    def a_first(role):
        def body(i, b):
            fill(AX + 4 * role, i, b, 1, [])
            item(AX + 4 * role, i, to_pair).start()

        each(4, lambda i: a_row(role, i), body)

    def a_mid():
        def body(i, b):
            item(AX, i, to_pair).wait_recv()
            fill(AX + 8, i, b, 1, [AX + i])
            item(AX + 8, i, to_next).start()

        each(4, lambda i: a_row(2, i), body)

    zk = jnp.where(odd, 1 - zl, zl)

    def b_slot(to):
        return BZ + 2 * jnp.where(to == x_far, 0, jnp.where(to == x_pair, 1, jnp.where(to == x_next, 2, 3)))

    def b_across(to):
        base = b_slot(to)

        def body(i, b):
            fill(base, i, b, 0, [])
            item(base, i, partner).start()

        each(2, lambda i: 4 * to + 2 * (1 - zk) + i, body)

    def b_first(role):
        def body(i, b):
            item(BZ + 2 * role, i, partner).wait_recv()
            fill(BX + 2 * role, i, b, 0, [BZ + 2 * role + i])
            item(BX + 2 * role, i, to_pair).start()

        each(2, lambda i: b_row(role, i, zk), body)

    def b_mid():
        def body(i, b):
            item(BZ + 4, i, partner).wait_recv()
            item(BX, i, to_pair).wait_recv()
            fill(BX + 4, i, b, 0, [BZ + 4 + i, BX + i])
            item(BX + 4, i, to_next).start()

        each(2, lambda i: b_row(2, i, zk), body)

    even = jnp.logical_not(odd)

    def a_home(z_from, z_to, i):
        slot = AZ + 2 * z_from + i
        to = (2 * x + z_to, swap_c)
        return remote(pout.at[AZ + 2 * z_to + i], pin.at[slot], p_send.at[AZ + 2 * z_to + i], p_recv.at[slot], to)

    def a_final(z_to, is_own):
        def body(i, b):
            item(AX + 4, 2 * z_to + i, to_pair).wait_recv()
            item(AX + 8, 2 * z_to + i, to_next).wait_recv()
            adds = [AX + 4 + 2 * z_to + i, AX + 8 + 2 * z_to + i]
            for k in range(8):
                rows = pl.ds(k * 64, 64)
                value = product(b, k, 1)
                for add in adds:
                    value = value + pin[add, rows, :].astype(jnp.float32)
                if is_own:
                    out_ref[pl.ds(i * 512 + k * 64, 64), 256:] = value
                pout[AZ + 2 * z_to + i, rows, :] = value.astype(jnp.bfloat16)

            @pl.when(odd)
            def _():
                a_home(zl, z_to, i).start()

            if not is_own:
                @pl.when(even)
                def _():
                    a_home(zl, z_to, i).start()

        each(2, lambda i: 4 * x + 2 * z_to + i, body)

    def b_home(i):
        return item(BS, i, (2 * x + zk, swap_c))

    def b_final():
        def body(i, b):
            item(BZ + 6, i, partner).wait_recv()
            item(BX + 2, i, to_pair).wait_recv()
            item(BX + 4, i, to_next).wait_recv()
            for k in range(8):
                rows = pl.ds(k * 64, 64)
                value = product(b, k, 0)
                for add in (BZ + 6 + i, BX + 2 + i, BX + 4 + i):
                    value = value + pin[add, rows, :].astype(jnp.float32)
                out_ref[pl.ds(i * 512 + k * 64, 64), :256] = value
                pout[BS + i, rows, :] = value.astype(jnp.bfloat16)

            @pl.when(odd)
            def _():
                b_home(i).start()

        each(2, lambda i: 4 * x + 2 * zk + i, body)

    def left(count, row, copy, when=None):
        def one(i, carry):
            live = row(i) <= vc
            if when is not None:
                live = jnp.logical_and(live, when)

            @pl.when(live)
            def _():
                copy(i).wait_send()

            return carry

        lax.fori_loop(0, count, one, 0)

    def gather_left():
        for copy in sent + col_copies:
            copy.wait_send()

    def rows_left():
        for kind in range(KINDS):
            ref = part(rows_at, c, 0 if kind in (4, 6, 11, 16) else None)
            remote(ref, ref, a_send.at[rows_at, kind], a_recv.at[rows_at, kind], sib).wait_send()

    def first_left():
        for role in range(3):
            left(4, lambda i: a_row(role, i), lambda i: item(AX + 4 * role, i, to_pair))
        for role in range(4):
            left(2, lambda i: b_row(role, i, 1 - zk), lambda i: item(BZ + 2 * role, i, partner))

    low_first = jnp.where(x >= 2, 0, 1)
    a_first(low_first)
    b_across(0)
    b_across(1)
    rows_step(near_on, cross_on, False)
    gather_left()
    rows_step(near_end, cross_end, False)
    pl.when(x < 2)(lambda: a_first(0))
    b_across(2)
    b_across(3)
    pl.when(x >= 2)(lambda: a_first(1))
    a_mid()
    b_first(low_first)
    b_first(1 - low_first)
    a_final(zl, True)
    a_final(1 - zl, False)
    rows_left()
    b_mid()
    first_left()
    b_final()

    for i in range(2):
        b = 2 * r + i
        rows = pl.ds(i * 512, 512)

        @pl.when(b > c)
        def _():
            out_ref[rows, :] = jnp.zeros((512, 512), jnp.float32)

        @pl.when(jnp.logical_and(even, b <= c))
        def _():
            a_home(1 - zl, zl, i).wait_recv()
            out_ref[rows, 256:] = out_ref[rows, 256:] + pin[AZ + 2 * (1 - zl) + i].astype(jnp.float32)

        @pl.when(jnp.logical_and(odd, b <= c))
        def _():
            a_home(0, zl, i).wait_recv()
            a_home(1, zl, i).wait_recv()
            out_ref[rows, 256:] = pin[AZ + i].astype(jnp.float32) + pin[AZ + 2 + i].astype(jnp.float32)

    for i in range(2):
        @pl.when(jnp.logical_and(odd, 2 * r + i <= c))
        def _():
            b_home(i).wait_recv()
            out_ref[pl.ds(i * 512, 512), :256] = pin[BS + i].astype(jnp.float32)

    for role in range(3):
        left(2, lambda i: b_row(role, i, zk), lambda i: item(BX + 2 * role, i, to_pair))
    left(2, lambda i: 4 * x + 2 * (1 - zl) + i, lambda i: a_home(zl, 1 - zl, i))
    left(2, lambda i: 4 * x + 2 * zl + i, lambda i: a_home(zl, zl, i), odd)
    left(2, lambda i: 4 * x + 2 * zk + i, b_home, odd)


def local(densities, screened, q_table):
    block_len, pair_count, g_slice = densities.shape
    d = densities.reshape(block_len * pair_count, g_slice)
    bf = jnp.bfloat16
    dma = pltpu.SemaphoreType.DMA
    return pl.pallas_call(
        kernel,
        out_shape=pltpu.VMEM((1024, 512), jnp.float32),
        in_specs=[
            pl.BlockSpec(memory_space=pl.ANY),
            pl.BlockSpec(memory_space=pl.ANY),
            pl.BlockSpec(memory_space=pl.ANY),
        ],
        out_specs=pl.BlockSpec(memory_space=pltpu.VMEM),
        scratch_shapes=[
            pltpu.SMEM((128, 128), jnp.int32),
            pltpu.VMEM((16, 16, 256, 128), bf),
            pltpu.VMEM((16, 512, 256), bf),
            pltpu.VMEM((8, 512, 256), bf),
            pltpu.VMEM((512, 256), bf),
            pltpu.VMEM((16, 512, 256), bf),
            pltpu.VMEM((ITEMS, 512, 256), bf),
            pltpu.VMEM((ITEMS, 512, 256), bf),
            pltpu.VMEM((SIZES[-1], 512, 256), jnp.float32),
            dma((5,)),
            dma((CHUNKS + 1, KINDS)),
            dma((CHUNKS + 1, KINDS)),
            dma((8,)),
            dma((8,)),
            dma((ITEMS,)),
            dma((ITEMS,)),
        ],
        compiler_params=pltpu.CompilerParams(
            collective_id=0, has_side_effects=True, vmem_limit_bytes=61 * 2**20
        ),
        cost_estimate=pl.CostEstimate(flops=10 * 10**9, bytes_accessed=4 * 2**20, transcendentals=0),
    )(d, screened, q_table)


def solution(mesh):
    return jax.shard_map(
        local,
        mesh=mesh,
        in_specs=(P("kc", None, "kr"), P(None, "kr", "kc"), P()),
        out_specs=P("kr", "kc"),
        check_vma=False,
    )
```
